32 devices in a mesh: dp: 8 (over y, x, core), mp: 4 (over z).
Axes of the slice: x: 2, y: 2, z: 4, core: 2. Of those that a mesh axis runs over, the one named last changes fastest.
Arguments:
- patches: bfloat16 [1024, 6144], P('dp', 'mp'), may hold values from -200 to 200
- norm_gain: float32 [6144], replicated, may hold values from 0.25 to 1.75
- value_weight: bfloat16 [6144, 3072], P(None, 'mp'), may hold values from -0.078125 to 0.078125
- queries: bfloat16 [1024, 3072], P('dp', 'mp'), may hold values from -100 to 100
- key_vectors: bfloat16 [1024, 3072], P('dp', 'mp'), may hold values from -4 to 4
- head_cotangent: bfloat16 [2048, 3072], P('dp', 'mp'), may hold values from -6 to 6
- image_owner: int32 [8, 8], replicated, may hold values from 0 to 7, as said below
- patch_count: int32 [8, 8], replicated, may hold values from 0 to 32, as said below
Outputs:
- value_grad: float32 [6144, 3072], P('dp', 'mp')
- query_grad: bfloat16 [1024, 3072], P('dp', 'mp')
- key_grad: bfloat16 [1024, 3072], P('dp', 'mp')
The draws below stay inside these ranges and needn't reach their ends.
Inputs may be any that keep to these rules, and one draw needn't show every extreme that they name: `image_owner`: each row lists every owner once. `patch_count`: 0 marks an empty image slot; each row sums to 128; some owner receives 32 patches from every device.
All inputs are finite; a program needn't handle non-finite values.
Results may differ from the reference program's by a relative error of at most 0.0065.
Values may be sent and summed in bfloat16 or wider, within the bound.
No kernel may reach another device: no remote copies, remote signals or barrier semaphores. Data moves between devices by JAX's collectives and lax.ppermute only.
A program may use at most 128 MiB of HBM per device.

```python
import math
import jax
import jax.numpy as jnp
from jax import lax

D = 6144
HEADS = 24
HD = 128
CAP = 32
ROWS_DEV = 128
SLOTS = 256
TOTAL_ROWS = 1024
N_DP = 8


def plan_tables(key):
    key_special = jax.random.fold_in(key, 101)
    key_portion = jax.random.fold_in(key, 102)
    key_order = jax.random.fold_in(key, 103)
    special = jax.random.randint(key_special, (), 0, N_DP)
    portion = jax.random.randint(key_portion, (N_DP, N_DP // 2), 0, CAP + 1)
    column = jnp.arange(N_DP // 2, dtype=jnp.int32)
    forced = jnp.where(special % 2 == 0, CAP, 0)
    portion = jnp.where(column[None, :] == special // 2, forced, portion)
    to_owner = jnp.stack([portion, CAP - portion], axis=2).reshape(N_DP, N_DP)
    order_keys = jax.random.split(key_order, N_DP)
    owners = jax.vmap(lambda single: jax.random.permutation(single, N_DP))(order_keys).astype(jnp.int32)
    counts = jnp.take_along_axis(to_owner, owners, axis=1).astype(jnp.int32)
    return (owners, counts)


def draw_image_owner(key, part):
    return plan_tables(key)[0]


def draw_patch_count(key, part):
    return plan_tables(key)[1]


def draw_patches(key, part):
    column_scale = jnp.exp(jax.random.uniform(jax.random.fold_in(key, 202), (D,), minval=math.log(0.5), maxval=math.log(5.0)))
    base = jnp.clip(jax.random.normal(jax.random.fold_in(key, 201), (TOTAL_ROWS, D)), -4.0, 4.0)
    row_scale = jnp.exp(jax.random.uniform(jax.random.fold_in(key, 203), (TOTAL_ROWS,), minval=math.log(0.5), maxval=math.log(5.0)))
    return (base * column_scale[None, :] * row_scale[:, None]).astype(jnp.bfloat16)


def query_key(key):
    key_part = jnp.clip(jax.random.normal(jax.random.fold_in(key, 301), (TOTAL_ROWS, HEADS * HD)), -4.0, 4.0)
    query_part = jnp.clip(jax.random.normal(jax.random.fold_in(key, 302), (TOTAL_ROWS, HEADS * HD)), -4.0, 4.0)
    return (query_part.astype(jnp.float32), key_part.astype(jnp.float32))


def draw_queries(key, part):
    return query_key(key)[0].astype(jnp.bfloat16)


def draw_key_vectors(key, part):
    return query_key(key)[1].astype(jnp.bfloat16)


def block_levels(stream_key, dims, cuts, low, top_value):
    def one(dim, blocks):
        steps = jax.random.uniform(jax.random.fold_in(jax.random.fold_in(stream_key, 6), dim), (blocks,), jnp.float32, low / len(cuts), top_value / len(cuts))
        return jnp.repeat(jnp.exp(steps), dims[dim] // blocks).reshape((-1,) + (1,) * (len(dims) - dim - 1))

    level = one(*cuts[0])
    for cut in cuts[1:]:
        level = level * one(*cut)
    return level


def noise(stream_key, dims, scale, reach, shards=(), kind=jnp.bfloat16):
    loudness = block_levels(stream_key, dims, shards, -0.22, 0.18) if shards else 1.0
    result = jax.random.normal(stream_key, dims, jnp.float32) * scale * loudness
    return jnp.minimum(jnp.maximum(result, -reach), reach).astype(kind)


def setup_inputs(seed: int = 0) -> dict:
    seeds = jax.random.split(jax.random.key(seed), 9)
    patches = draw_patches(jax.random.fold_in(seeds[8], 71), 0)
    norm_gain = jnp.clip(1.0 + 0.15 * jax.random.normal(seeds[1], (D,), jnp.float32), 0.25, 1.75)
    value_weight = noise(seeds[2], (D, HEADS * HD), D ** -0.5, 0.078125, ((1, 4),))
    queries = draw_queries(jax.random.fold_in(seeds[8], 71), 0)
    key_vectors = draw_key_vectors(jax.random.fold_in(seeds[8], 71), 0)
    head_cotangent = noise(seeds[5], (N_DP * SLOTS, HEADS * HD), 1.0, 6.0, ((0, 8), (1, 4)))
    image_owner = draw_image_owner(jax.random.fold_in(seeds[8], 71), 0)
    patch_count = draw_patch_count(jax.random.fold_in(seeds[8], 71), 0)
    return {"patches": patches, "norm_gain": norm_gain, "value_weight": value_weight, "queries": queries, "key_vectors": key_vectors, "head_cotangent": head_cotangent, "image_owner": image_owner, "patch_count": patch_count}


def normalize(rows, norm_gain):
    values = rows.astype(jnp.float32)
    average = lax.optimization_barrier(jnp.mean(values, axis=-1, keepdims=True))
    centred = values - average
    variance = lax.optimization_barrier(jnp.mean(centred * centred, axis=-1, keepdims=True))
    return (centred * lax.rsqrt(variance + 1e-06) * norm_gain).astype(jnp.bfloat16)

def attention_grads(query_rows, key_rows, value_rows, cotangent, segment):
    total = query_rows.shape[0]
    heads_here = query_rows.shape[1] // HD
    scale = HD ** (-0.5)
    query_heads = query_rows.reshape(total, heads_here, HD).astype(jnp.float32)
    key_heads = key_rows.reshape(total, heads_here, HD).astype(jnp.float32)
    value_heads = value_rows.reshape(total, heads_here, HD).astype(jnp.float32)
    cot_heads = cotangent.reshape(total, heads_here, HD).astype(jnp.float32)
    scores = jnp.einsum('qhd,khd->hqk', query_heads, key_heads) * scale
    allowed = segment[:, None] == segment[None, :]
    scores = jnp.where(allowed[None], scores, -1000000000.0)
    peak = lax.optimization_barrier(jnp.max(scores, axis=-1, keepdims=True))
    weights = jnp.exp(scores - peak)
    weights = weights / lax.optimization_barrier(jnp.sum(weights, axis=-1, keepdims=True))
    rounded = weights.astype(jnp.bfloat16).astype(jnp.float32)
    value_grad = jnp.einsum('hqk,qhd->khd', rounded, cot_heads).astype(jnp.bfloat16)
    prob_grad = jnp.einsum('qhd,khd->hqk', cot_heads, value_heads)
    centre = lax.optimization_barrier(jnp.sum(weights * prob_grad, axis=-1, keepdims=True))
    score_grad = (weights * (prob_grad - centre)).astype(jnp.bfloat16).astype(jnp.float32)
    query_grad = (jnp.einsum('hqk,khd->qhd', score_grad, key_heads) * scale).astype(jnp.bfloat16)
    key_grad = (jnp.einsum('hqk,qhd->khd', score_grad, query_heads) * scale).astype(jnp.bfloat16)
    width = heads_here * HD
    return (value_grad.reshape(total, width), query_grad.reshape(total, width), key_grad.reshape(total, width))

def reference(patches, norm_gain, value_weight, queries, key_vectors, head_cotangent, image_owner, patch_count):

    def one_source(source):
        first = (source * ROWS_DEV).astype(jnp.int32)
        rows = lax.dynamic_slice_in_dim(patches, first, ROWS_DEV, 0)
        query_rows = lax.dynamic_slice_in_dim(queries, first, ROWS_DEV, 0)
        key_rows = lax.dynamic_slice_in_dim(key_vectors, first, ROWS_DEV, 0)
        own_list = lax.dynamic_index_in_dim(image_owner, source, 0, keepdims=False).astype(jnp.int32)
        own_count = lax.dynamic_index_in_dim(patch_count, source, 0, keepdims=False).astype(jnp.int32)
        ends = jnp.cumsum(own_count).astype(jnp.int32)
        starts = (ends - own_count).astype(jnp.int32)
        row_index = jnp.arange(ROWS_DEV, dtype=jnp.int32)
        image_of = lax.optimization_barrier(jnp.sum((ends[None, :] <= row_index[:, None]).astype(jnp.int32), axis=1)).astype(jnp.int32)
        picked = image_of[:, None] == jnp.arange(N_DP, dtype=jnp.int32)[None, :]
        row_owner = lax.optimization_barrier(jnp.sum(jnp.where(picked, own_list[None, :], 0), axis=1)).astype(jnp.int32)
        row_start = lax.optimization_barrier(jnp.sum(jnp.where(picked, starts[None, :], 0), axis=1)).astype(jnp.int32)
        packed_index = (row_owner * SLOTS + source * CAP + row_index - row_start).astype(jnp.int32)
        cotangent = head_cotangent[packed_index]
        normed = normalize(rows, norm_gain)
        value_rows = jnp.dot(normed, value_weight, preferred_element_type=jnp.float32).astype(jnp.bfloat16)
        value_grad, query_grad, key_grad = attention_grads(query_rows, key_rows, value_rows, cotangent, image_of)
        return (normed, value_grad, query_grad, key_grad)
    normed, value_rows, query_grad, key_grad = lax.map(one_source, jnp.arange(N_DP, dtype=jnp.int32))
    normed = normed.reshape(TOTAL_ROWS, D)
    value_rows = value_rows.reshape(TOTAL_ROWS, HEADS * HD)
    weight_grad = jnp.dot(normed.T, value_rows, preferred_element_type=jnp.float32)
    return (weight_grad, query_grad.reshape(TOTAL_ROWS, HEADS * HD), key_grad.reshape(TOTAL_ROWS, HEADS * HD))
```

```python
import jax
import jax.numpy as jnp
from jax import lax
from jax.sharding import PartitionSpec as P

HD = 128


def normalize(rows, norm_gain):
    values = rows.astype(jnp.float32)
    average = jnp.mean(values, axis=-1, keepdims=True)
    centred = values - average
    variance = jnp.mean(centred * centred, axis=-1, keepdims=True)
    return (centred * lax.rsqrt(variance + 1e-06) * norm_gain).astype(jnp.bfloat16)


def row_plan(image_owner, patch_count, rows_here, capacity, devices):
    device = lax.axis_index("dp")
    own_list = lax.dynamic_index_in_dim(image_owner, device, 0, keepdims=False)
    own_count = lax.dynamic_index_in_dim(patch_count, device, 0, keepdims=False)
    ends = jnp.cumsum(own_count)
    starts = ends - own_count
    row_index = jnp.arange(rows_here, dtype=jnp.int32)
    image_of = jnp.sum((ends[None, :] <= row_index[:, None]).astype(jnp.int32), axis=1)
    picked = image_of[:, None] == jnp.arange(devices, dtype=jnp.int32)[None, :]
    row_owner = jnp.sum(jnp.where(picked, own_list[None, :], 0), axis=1)
    row_start = jnp.sum(jnp.where(picked, starts[None, :], 0), axis=1)
    return image_of, row_owner * capacity + row_index - row_start


def attention_grads(query_rows, key_rows, value_rows, cotangent, segment):
    total, width = query_rows.shape
    heads = width // HD
    scale = HD ** (-0.5)

    def split(rows):
        return rows.reshape(total, heads, HD)

    query, key, value, cot = split(query_rows), split(key_rows), split(value_rows), split(cotangent)
    scores = jnp.einsum("qhd,khd->hqk", query, key, preferred_element_type=jnp.float32) * scale
    allowed = segment[:, None] == segment[None, :]
    scores = jnp.where(allowed[None], scores, -1000000000.0)
    weights = jnp.exp(scores - jnp.max(scores, axis=-1, keepdims=True))
    weights = weights / jnp.sum(weights, axis=-1, keepdims=True)
    value_grad = jnp.einsum(
        "hqk,qhd->khd", weights.astype(jnp.bfloat16), cot, preferred_element_type=jnp.float32
    )
    prob_grad = jnp.einsum("qhd,khd->hqk", cot, value, preferred_element_type=jnp.float32)
    centre = jnp.sum(weights * prob_grad, axis=-1, keepdims=True)
    score_grad = (weights * (prob_grad - centre)).astype(jnp.bfloat16)
    query_grad = jnp.einsum("hqk,khd->qhd", score_grad, key, preferred_element_type=jnp.float32)
    key_grad = jnp.einsum("hqk,qhd->khd", score_grad, query, preferred_element_type=jnp.float32)

    def join(rows):
        return rows.astype(jnp.bfloat16).reshape(total, width)

    return join(value_grad), join(query_grad * scale), join(key_grad * scale)


def general_body(
    patches, norm_gain, value_weight, queries, key_vectors, head_cotangent, image_owner, patch_count
):
    devices = lax.axis_size("dp")
    rows_here = patches.shape[0]
    width = queries.shape[1]
    capacity = head_cotangent.shape[0] // devices
    segment, index = row_plan(image_owner, patch_count, rows_here, capacity, devices)
    slots = lax.all_to_all(
        head_cotangent.reshape(devices, capacity, width), "dp", split_axis=0, concat_axis=0, tiled=True
    )
    cotangent = slots.reshape(devices * capacity, width)[index]
    normed = normalize(lax.all_gather(patches, "mp", axis=1, tiled=True), norm_gain)
    values = jnp.dot(normed, value_weight, preferred_element_type=jnp.float32).astype(jnp.bfloat16)
    value_rows, query_grad, key_grad = attention_grads(
        queries, key_vectors, values, cotangent, segment
    )
    all_value_rows = lax.all_gather(value_rows, "dp", axis=0, tiled=True)
    columns = jnp.swapaxes(normed.reshape(rows_here, devices, -1), 0, 1)
    columns = lax.all_to_all(columns, "dp", split_axis=0, concat_axis=0, tiled=True)
    columns = columns.reshape(devices * rows_here, -1)
    weight_grad = lax.dot_general(
        columns, all_value_rows, (((0,), (0,)), ((), ())), preferred_element_type=jnp.float32
    )
    return weight_grad, query_grad, key_grad


def solution(mesh):
    return jax.shard_map(
        general_body,
        mesh=mesh,
        in_specs=(
            P("dp", "mp"),
            P(),
            P(None, "mp"),
            P("dp", "mp"),
            P("dp", "mp"),
            P("dp", "mp"),
            P(),
            P(),
        ),
        out_specs=(P("dp", "mp"), P("dp", "mp"), P("dp", "mp")),
        check_vma=False,
    )
```

```python
import functools

import jax
import jax.numpy as jnp
from jax import lax
from jax.experimental import pallas as pl
from jax.experimental.pallas import tpu as pltpu
from jax.sharding import PartitionSpec as P

HD = 128
EXTRA = 16


def normalize(rows, norm_gain):
    values = rows.astype(jnp.float32)
    average = jnp.mean(values, axis=-1, keepdims=True)
    centred = values - average
    variance = jnp.mean(centred * centred, axis=-1, keepdims=True)
    return (centred * lax.rsqrt(variance + 1e-06) * norm_gain).astype(jnp.bfloat16)


def row_plan(image_owner, patch_count, rows_here, capacity, devices):
    device = lax.axis_index("dp")
    own_list = lax.dynamic_index_in_dim(image_owner, device, 0, keepdims=False)
    own_count = lax.dynamic_index_in_dim(patch_count, device, 0, keepdims=False)
    ends = jnp.cumsum(own_count)
    starts = ends - own_count
    row_index = jnp.arange(rows_here, dtype=jnp.int32)
    image_of = jnp.sum((ends[None, :] <= row_index[:, None]).astype(jnp.int32), axis=1)
    picked = image_of[:, None] == jnp.arange(devices, dtype=jnp.int32)[None, :]
    row_owner = jnp.sum(jnp.where(picked, own_list[None, :], 0), axis=1)
    row_start = jnp.sum(jnp.where(picked, starts[None, :], 0), axis=1)
    return image_of, row_owner * capacity + row_index - row_start


def attention_grads(query_rows, key_rows, value_rows, cotangent, segment):
    total, width = query_rows.shape
    heads = width // HD
    scale = HD ** (-0.5)

    def split(rows):
        return rows.reshape(total, heads, HD)

    query, key, value, cot = split(query_rows), split(key_rows), split(value_rows), split(cotangent)
    scores = jnp.einsum("qhd,khd->hqk", query, key, preferred_element_type=jnp.float32) * scale
    allowed = segment[:, None] == segment[None, :]
    scores = jnp.where(allowed[None], scores, -1000000000.0)
    weights = jnp.exp(scores - jnp.max(scores, axis=-1, keepdims=True))
    weights = weights / jnp.sum(weights, axis=-1, keepdims=True)
    value_grad = jnp.einsum(
        "hqk,qhd->khd", weights.astype(jnp.bfloat16), cot, preferred_element_type=jnp.float32
    )
    prob_grad = jnp.einsum("qhd,khd->hqk", cot, value, preferred_element_type=jnp.float32)
    centre = jnp.sum(weights * prob_grad, axis=-1, keepdims=True)
    score_grad = (weights * (prob_grad - centre)).astype(jnp.bfloat16)
    query_grad = jnp.einsum("hqk,khd->qhd", score_grad, key, preferred_element_type=jnp.float32)
    key_grad = jnp.einsum("hqk,qhd->khd", score_grad, query, preferred_element_type=jnp.float32)

    def join(rows):
        return rows.astype(jnp.bfloat16).reshape(total, width)

    return join(value_grad), join(query_grad * scale), join(key_grad * scale)


def general_body(
    patches, norm_gain, value_weight, queries, key_vectors, head_cotangent, image_owner, patch_count
):
    devices = lax.axis_size("dp")
    rows_here = patches.shape[0]
    width = queries.shape[1]
    capacity = head_cotangent.shape[0] // devices
    segment, index = row_plan(image_owner, patch_count, rows_here, capacity, devices)
    slots = lax.all_to_all(
        head_cotangent.reshape(devices, capacity, width), "dp", split_axis=0, concat_axis=0, tiled=True
    )
    cotangent = slots.reshape(devices * capacity, width)[index]
    normed = normalize(lax.all_gather(patches, "mp", axis=1, tiled=True), norm_gain)
    values = jnp.dot(normed, value_weight, preferred_element_type=jnp.float32).astype(jnp.bfloat16)
    value_rows, query_grad, key_grad = attention_grads(
        queries, key_vectors, values, cotangent, segment
    )
    all_value_rows = lax.all_gather(value_rows, "dp", axis=0, tiled=True)
    columns = jnp.swapaxes(normed.reshape(rows_here, devices, -1), 0, 1)
    columns = lax.all_to_all(columns, "dp", split_axis=0, concat_axis=0, tiled=True)
    columns = columns.reshape(devices * rows_here, -1)
    weight_grad = lax.dot_general(
        columns, all_value_rows, (((0,), (0,)), ((), ())), preferred_element_type=jnp.float32
    )
    return weight_grad, query_grad, key_grad


def split3(value):
    high = value.astype(jnp.bfloat16)
    rest = value - high.astype(jnp.float32)
    middle = rest.astype(jnp.bfloat16)
    low = (rest - middle.astype(jnp.float32)).astype(jnp.bfloat16)
    return high, middle, low


def pre_kernel(place, x_ref, own_ref, other_ref):
    core = place[1]
    rows, columns = x_ref.shape
    half = columns // 2
    values = x_ref[...].astype(jnp.float32)
    mean = jnp.sum(values, axis=-1, keepdims=True) * (1.0 / columns)
    centred = values - mean
    spread = jnp.sum(centred * centred, axis=-1, keepdims=True)

    @pl.when(core == 0)
    def _():
        own_ref[:rows, :] = x_ref[:, :half]
        other_ref[...] = x_ref[:, half:]

    @pl.when(core == 1)
    def _():
        own_ref[:rows, :] = x_ref[:, half:]
        other_ref[...] = x_ref[:, :half]

    lane = lax.broadcasted_iota(jnp.int32, (rows, 128), 1)
    table = jnp.zeros((rows, 128), jnp.float32)
    for index, part in enumerate(split3(mean) + split3(spread)):
        table = jnp.where(lane == index, part.astype(jnp.float32), table)
    own_ref[rows:, :] = jnp.zeros((EXTRA, half), jnp.bfloat16)
    own_ref[rows:, :rows] = table.T[:EXTRA, :].astype(jnp.bfloat16)


def image_plan(owner_ref, count_ref, device, row, images, capacity):
    image = jnp.zeros(row.shape, jnp.int32)
    position = jnp.zeros(row.shape, jnp.int32)
    start = jnp.int32(0)
    for index in range(images):
        end = start + count_ref[device, index]
        inside = (row >= start) & (row < end)
        image = jnp.where(inside, index, image)
        position = jnp.where(inside, owner_ref[device, index] * capacity + row - start, position)
        start = end
    return image, position


def weights_kernel(images, place, owner_ref, count_ref, query_ref, key_ref, weights_ref):
    rows, width = query_ref.shape
    device = place[0] * 2 + place[1]
    down = lax.broadcasted_iota(jnp.int32, (rows, rows), 0)
    across = lax.broadcasted_iota(jnp.int32, (rows, rows), 1)
    image_down, _ = image_plan(owner_ref, count_ref, device, down, images, 1)
    image_across, _ = image_plan(owner_ref, count_ref, device, across, images, 1)
    allowed = image_down == image_across
    for head in range(width // HD):
        columns = slice(head * HD, (head + 1) * HD)
        scores = lax.dot_general(
            query_ref[:, columns], key_ref[:, columns], (((1,), (1,)), ((), ())),
            preferred_element_type=jnp.float32,
        ) * (HD ** (-0.5))
        scores = jnp.where(allowed, scores, -1000000000.0)
        weights = jnp.exp(scores - jnp.max(scores, axis=-1, keepdims=True))
        weights_ref[head] = weights / jnp.sum(weights, axis=-1, keepdims=True)


def value_kernel(images, place, owner_ref, count_ref, slots_ref, weights_ref, cot_ref, value_ref):
    slots, width = slots_ref.shape
    rows = cot_ref.shape[0]
    device = place[0] * 2 + place[1]
    row = lax.broadcasted_iota(jnp.int32, (rows, slots), 0)
    _, position = image_plan(owner_ref, count_ref, device, row, images, slots // images)
    pick = position == lax.broadcasted_iota(jnp.int32, (rows, slots), 1)
    pick = jnp.where(pick, 1.0, 0.0).astype(jnp.bfloat16)
    cot_ref[...] = jnp.dot(
        pick, slots_ref[...], preferred_element_type=jnp.float32
    ).astype(jnp.bfloat16)
    for head in range(width // HD):
        columns = slice(head * HD, (head + 1) * HD)
        value_ref[:, columns] = lax.dot_general(
            weights_ref[head].astype(jnp.bfloat16), cot_ref[:, columns], (((0,), (0,)), ((), ())),
            preferred_element_type=jnp.float32,
        ).astype(jnp.bfloat16)


def column_stats(mean, rstd):
    rows = mean.shape[1]
    both = jnp.concatenate([mean, rstd, jnp.zeros((126, rows), jnp.float32)], axis=0).T
    return both[:, 0:1], both[:, 1:2]


def norm_kernel(
    first, place, gain_ref, stats_in, own, one, two, near, far, *rest
):
    if first:
        stats_out, all_ref, x_ref, y_ref, xy_ref, source, sems = rest
    else:
        all_ref, x_ref, y_ref, xy_ref, source, sems = rest
    chip, core, layer = place[0], place[1], place[2]
    outer = (layer == 0) | (layer == 3)
    rows = x_ref.shape[0]
    for index, ref in enumerate((own, one, two)):
        pltpu.make_async_copy(ref, source.at[index], sems.at[index]).start()

    @pl.when(outer)
    def _():
        pltpu.make_async_copy(far, source.at[3], sems.at[3]).start()

    @pl.when(jnp.logical_not(outer))
    def _():
        pltpu.make_async_copy(near, source.at[3], sems.at[3]).start()

    for index, ref in enumerate((own, one, two, far)):
        pltpu.make_async_copy(ref, source.at[index], sems.at[index]).wait()

    if first:
        means, spreads = [], []
        for index in range(4):
            part = source[index, rows:, :rows].astype(jnp.float32)
            means.append(part[0:1] + part[1:2] + part[2:3])
            spreads.append(part[3:4] + part[4:5] + part[5:6])
        mean = (means[0] + means[1] + means[2] + means[3]) * 0.25
        shift = sum((part - mean) * (part - mean) for part in means)
        columns = 2 * x_ref.shape[1]
        spread = spreads[0] + spreads[1] + spreads[2] + spreads[3] + shift * columns
        rstd = lax.rsqrt(spread * (1.0 / (4 * columns)) + 1e-06)
        stats_out[...] = jnp.concatenate([mean, rstd, jnp.zeros((6, rows), jnp.float32)], axis=0)
    else:
        mean, rstd = stats_in[0:1, :], stats_in[1:2, :]
    mean, rstd = column_stats(mean, rstd)
    for offset, ref in enumerate((None, x_ref, y_ref, xy_ref)):
        block = chip ^ offset
        values = source[block ^ layer, :rows, :].astype(jnp.float32)
        gain = gain_ref[pl.ds(2 * block + core, 1), :]
        normed = ((values - mean) * rstd * gain).astype(jnp.bfloat16)
        all_ref[offset] = normed
        if ref is not None:
            ref[...] = normed


def project_kernel(order, normed_ref, weight_ref, total_ref):
    part = jnp.dot(normed_ref[0], weight_ref[...], preferred_element_type=jnp.float32)

    @pl.when(pl.program_id(0) == 0)
    def _():
        total_ref[...] = part

    @pl.when(pl.program_id(0) > 0)
    def _():
        total_ref[...] += part


def backward_kernel(
    order, normed_ref, weight_ref, first_ref, query_ref, key_ref, cot_ref, weights_ref, query_out, key_out, total
):
    step = pl.program_id(0)
    part = jnp.dot(normed_ref[0], weight_ref[...], preferred_element_type=jnp.float32)

    @pl.when(step == 0)
    def _():
        total[...] = first_ref[...] + part

    @pl.when(step > 0)
    def _():
        total[...] += part

    @pl.when(step == pl.num_programs(0) - 1)
    def _():
        scale = HD ** (-0.5)
        for head in range(query_ref.shape[1] // HD):
            columns = slice(head * HD, (head + 1) * HD)
            values = total[:, columns].astype(jnp.bfloat16)
            weights = weights_ref[head]
            prob_grad = lax.dot_general(
                cot_ref[:, columns], values, (((1,), (1,)), ((), ())), preferred_element_type=jnp.float32
            )
            centre = jnp.sum(weights * prob_grad, axis=-1, keepdims=True)
            score_grad = (weights * (prob_grad - centre)).astype(jnp.bfloat16)
            query_out[:, columns] = (
                jnp.dot(score_grad, key_ref[:, columns], preferred_element_type=jnp.float32) * scale
            ).astype(jnp.bfloat16)
            key_out[:, columns] = (
                lax.dot_general(
                    score_grad, query_ref[:, columns], (((0,), (0,)), ((), ())),
                    preferred_element_type=jnp.float32,
                ) * scale
            ).astype(jnp.bfloat16)


def gradient_kernel(*refs):
    n0, n1, n2, n3, v0, v1, v2, v3 = refs[:8]
    normed = jnp.concatenate([n0[0], n1[...], n2[...], n3[...]], axis=0)
    values = jnp.concatenate([v0[...], v1[...], v2[...], v3[...]], axis=0)
    part = lax.dot_general(
        normed, values, (((0,), (0,)), ((), ())), preferred_element_type=jnp.float32
    )
    if len(refs) == 10:
        refs[9][...] = refs[8][...] + part
    else:
        refs[8][...] = part


def shape(dims, dtype=jnp.bfloat16):
    return jax.ShapeDtypeStruct(dims, dtype)


def cost(flops, moved):
    return pl.CostEstimate(flops=flops, bytes_accessed=moved, transcendentals=0)


VMEM_LIMIT = 40 * 1024 * 1024
SMEM = pl.BlockSpec(memory_space=pltpu.SMEM)
WHOLE = pl.BlockSpec(memory_space=pltpu.VMEM)
ANY = pl.BlockSpec(memory_space=pl.ANY)


def call(kernel, name, out_shape, in_specs, out_specs, flops, moved, scratch=()):
    return pl.pallas_call(
        kernel,
        name=name,
        out_shape=out_shape,
        in_specs=in_specs,
        out_specs=out_specs,
        scratch_shapes=list(scratch),
        cost_estimate=cost(flops, moved),
        compiler_params=pltpu.CompilerParams(vmem_limit_bytes=VMEM_LIMIT),
    )


def across(rows, distance):
    return lax.ppermute(rows, "dp", [(i, i ^ distance) for i in range(8)])


def line_gather(rows):
    one = lax.ppermute(rows, "mp", [(0, 1), (1, 0), (2, 3), (3, 2)])
    two = lax.ppermute(rows, "mp", [(0, 2), (2, 0), (1, 3), (3, 1)])
    near = lax.ppermute(rows, "mp", [(1, 2), (2, 1)])
    far = lax.ppermute(two, "mp", [(2, 3), (1, 0)])
    return one, two, near, far


def fast_body(
    patches, norm_gain, value_weight, queries, key_vectors, head_cotangent, image_owner, patch_count
):
    rows, columns = patches.shape
    half = columns // 2
    width = queries.shape[1]
    heads = width // HD
    images = image_owner.shape[1]
    slots = head_cotangent.shape[0]
    device = lax.axis_index("dp").astype(jnp.int32)
    chip, core, layer = device // 2, device % 2, lax.axis_index("mp").astype(jnp.int32)
    place = jnp.stack([chip, core, layer])
    block = shape((rows, half))

    own, other = call(
        pre_kernel, "split_rows", (shape((rows + EXTRA, half)), block), [SMEM, WHOLE], (WHOLE, WHOLE),
        rows * columns * 6, rows * columns * 4,
    )(place, patches)
    received = lax.all_to_all(
        head_cotangent.reshape(8, slots // 8, width), "dp", split_axis=0, concat_axis=0, tiled=True
    ).reshape(slots, width)
    first = line_gather(own)
    mate = across(other, 1)
    second = line_gather(mate)

    weights = call(
        functools.partial(weights_kernel, images), "attention_weights",
        shape((heads, rows, rows), jnp.float32), [SMEM] * 3 + [WHOLE] * 2, WHOLE,
        rows * rows * width * 2, rows * width * 8,
    )(place, image_owner, patch_count, queries, key_vectors)
    cotangent, value_rows = call(
        functools.partial(value_kernel, images), "value_rows",
        (shape((rows, width)), shape((rows, width))), [SMEM] * 3 + [WHOLE] * 2, (WHOLE, WHOLE),
        rows * rows * width * 6, rows * width * 10,
    )(place, image_owner, patch_count, received, weights)
    chip_values = [value_rows] + [across(value_rows, distance) for distance in (2, 4, 6)]
    mate_values = [across(part, 1) for part in chip_values]

    gain = norm_gain.reshape(8, half)
    stats_shape = shape((8, rows), jnp.float32)
    stack = shape((4, rows, half))

    def norm(is_first, stats, own_rows, gathered):
        height = own_rows.shape[0]
        outs = ((stats_shape,) if is_first else ()) + (stack, block, block, block)
        return call(
            functools.partial(norm_kernel, is_first), "norm_columns",
            outs, [SMEM, WHOLE, WHOLE] + [ANY] * 5, (WHOLE,) * len(outs),
            rows * half * 24, rows * half * 24,
            (pltpu.VMEM((4, height, half), jnp.bfloat16), pltpu.SemaphoreType.DMA((4,))),
        )(place, gain, stats, own_rows, *gathered)

    def exchange(blocks):
        return [across(part, distance) for part, distance in zip(blocks, (2, 4, 6))]

    stats, first_all, *first_blocks = norm(True, jnp.zeros((8, rows), jnp.float32), own, first)
    mate_stats = across(stats, 1)
    first_columns = exchange(first_blocks)
    second_all, *second_blocks = norm(False, mate_stats, mate, second)
    second_columns = exchange(second_blocks)
    other_all = across(second_all, 1)

    offsets = jnp.arange(4, dtype=jnp.int32)
    order = (chip ^ offsets) * 2
    step_specs = [
        pl.BlockSpec((1, rows, half), lambda j, order: (j, 0, 0)),
        pl.BlockSpec((half, width), lambda j, order: (order[j], 0)),
    ]

    def full(dims):
        return pl.BlockSpec(dims, lambda j, order: (0,) * len(dims))

    flat = (rows, width)
    total = pl.pallas_call(
        project_kernel, name="project_own_half",
        grid_spec=pltpu.PrefetchScalarGridSpec(
            num_scalar_prefetch=1, grid=(4,), in_specs=step_specs, out_specs=full(flat)
        ),
        out_shape=shape(flat, jnp.float32),
        cost_estimate=cost(rows * half * 8 * width, half * width * 8),
        compiler_params=pltpu.CompilerParams(vmem_limit_bytes=VMEM_LIMIT),
    )(order + core, first_all, value_weight)
    query_grad, key_grad = pl.pallas_call(
        backward_kernel, name="attention_backward",
        grid_spec=pltpu.PrefetchScalarGridSpec(
            num_scalar_prefetch=1, grid=(4,),
            in_specs=step_specs + [full(flat)] * 4 + [full((heads, rows, rows))],
            out_specs=(full(flat), full(flat)),
            scratch_shapes=[pltpu.VMEM(flat, jnp.float32)],
        ),
        out_shape=(shape(flat), shape(flat)),
        cost_estimate=cost(rows * half * 10 * width, half * width * 8),
        compiler_params=pltpu.CompilerParams(vmem_limit_bytes=VMEM_LIMIT),
    )(order + 1 - core, other_all, value_weight, total, queries, key_vectors, cotangent, weights)

    grad_shape = shape((half, width), jnp.float32)
    grad_cost = (8 * rows * half * width, 8 * rows * (half + width) + 8 * half * width)
    partial_grad = call(
        gradient_kernel, "gradient_first", grad_shape, [WHOLE] * 8, WHOLE, *grad_cost
    )(first_all, *first_columns, *chip_values)
    weight_grad = call(
        gradient_kernel, "gradient_second", grad_shape, [WHOLE] * 9, WHOLE, *grad_cost
    )(second_all, *second_columns, *mate_values, partial_grad)
    return weight_grad, query_grad, key_grad


def solution(mesh):
    fast = mesh.shape["dp"] == 8 and mesh.shape["mp"] == 4
    return jax.shard_map(
        fast_body if fast else general_body,
        mesh=mesh,
        in_specs=(
            P("dp", "mp"),
            P(),
            P(None, "mp"),
            P("dp", "mp"),
            P("dp", "mp"),
            P("dp", "mp"),
            P(),
            P(),
        ),
        out_specs=(P("dp", "mp"), P("dp", "mp"), P("dp", "mp")),
        check_vma=False,
    )
```

```python
import functools

import jax
import jax.numpy as jnp
from jax import lax
from jax.experimental import pallas as pl
from jax.experimental.pallas import tpu as pltpu
from jax.sharding import PartitionSpec as P

HD = 128
HEADER = 8
LATE = (1, 3, 5)


def normalize(rows, norm_gain):
    values = rows.astype(jnp.float32)
    average = jnp.mean(values, axis=-1, keepdims=True)
    centred = values - average
    variance = jnp.mean(centred * centred, axis=-1, keepdims=True)
    return (centred * lax.rsqrt(variance + 1e-06) * norm_gain).astype(jnp.bfloat16)


def row_plan(image_owner, patch_count, rows_here, capacity, devices):
    device = lax.axis_index("dp")
    own_list = lax.dynamic_index_in_dim(image_owner, device, 0, keepdims=False)
    own_count = lax.dynamic_index_in_dim(patch_count, device, 0, keepdims=False)
    ends = jnp.cumsum(own_count)
    starts = ends - own_count
    row_index = jnp.arange(rows_here, dtype=jnp.int32)
    image_of = jnp.sum((ends[None, :] <= row_index[:, None]).astype(jnp.int32), axis=1)
    picked = image_of[:, None] == jnp.arange(devices, dtype=jnp.int32)[None, :]
    row_owner = jnp.sum(jnp.where(picked, own_list[None, :], 0), axis=1)
    row_start = jnp.sum(jnp.where(picked, starts[None, :], 0), axis=1)
    return image_of, row_owner * capacity + row_index - row_start


def attention_grads(query_rows, key_rows, value_rows, cotangent, segment):
    total, width = query_rows.shape
    heads = width // HD
    scale = HD ** (-0.5)

    def split(rows):
        return rows.reshape(total, heads, HD)

    query, key, value, cot = split(query_rows), split(key_rows), split(value_rows), split(cotangent)
    scores = jnp.einsum("qhd,khd->hqk", query, key, preferred_element_type=jnp.float32) * scale
    allowed = segment[:, None] == segment[None, :]
    scores = jnp.where(allowed[None], scores, -1000000000.0)
    weights = jnp.exp(scores - jnp.max(scores, axis=-1, keepdims=True))
    weights = weights / jnp.sum(weights, axis=-1, keepdims=True)
    value_grad = jnp.einsum(
        "hqk,qhd->khd", weights.astype(jnp.bfloat16), cot, preferred_element_type=jnp.float32
    )
    prob_grad = jnp.einsum("qhd,khd->hqk", cot, value, preferred_element_type=jnp.float32)
    centre = jnp.sum(weights * prob_grad, axis=-1, keepdims=True)
    score_grad = (weights * (prob_grad - centre)).astype(jnp.bfloat16)
    query_grad = jnp.einsum("hqk,khd->qhd", score_grad, key, preferred_element_type=jnp.float32)
    key_grad = jnp.einsum("hqk,qhd->khd", score_grad, query, preferred_element_type=jnp.float32)

    def join(rows):
        return rows.astype(jnp.bfloat16).reshape(total, width)

    return join(value_grad), join(query_grad * scale), join(key_grad * scale)


def general_body(
    patches, norm_gain, value_weight, queries, key_vectors, head_cotangent, image_owner, patch_count
):
    devices = lax.axis_size("dp")
    rows_here = patches.shape[0]
    width = queries.shape[1]
    capacity = head_cotangent.shape[0] // devices
    segment, index = row_plan(image_owner, patch_count, rows_here, capacity, devices)
    slots = lax.all_to_all(
        head_cotangent.reshape(devices, capacity, width), "dp", split_axis=0, concat_axis=0, tiled=True
    )
    cotangent = slots.reshape(devices * capacity, width)[index]
    normed = normalize(lax.all_gather(patches, "mp", axis=1, tiled=True), norm_gain)
    values = jnp.dot(normed, value_weight, preferred_element_type=jnp.float32).astype(jnp.bfloat16)
    value_rows, query_grad, key_grad = attention_grads(
        queries, key_vectors, values, cotangent, segment
    )
    all_value_rows = lax.all_gather(value_rows, "dp", axis=0, tiled=True)
    columns = jnp.swapaxes(normed.reshape(rows_here, devices, -1), 0, 1)
    columns = lax.all_to_all(columns, "dp", split_axis=0, concat_axis=0, tiled=True)
    columns = columns.reshape(devices * rows_here, -1)
    weight_grad = lax.dot_general(
        columns, all_value_rows, (((0,), (0,)), ((), ())), preferred_element_type=jnp.float32
    )
    return weight_grad, query_grad, key_grad


def image_plan(info, row, images, capacity):
    image = jnp.zeros(row.shape, jnp.int32)
    position = jnp.zeros(row.shape, jnp.int32)
    start = jnp.int32(0)
    for index in range(images):
        end = start + info[HEADER + images + index]
        inside = (row >= start) & (row < end)
        image = jnp.where(inside, index, image)
        position = jnp.where(inside, info[HEADER + index] * capacity + row - start, position)
        start = end
    return image, position


def weights_kernel(images, info, gain_in, query_ref, key_ref, weights_ref, gain_ref):
    gain_ref[...] = gain_in[...]
    rows, width = query_ref.shape
    down = lax.broadcasted_iota(jnp.int32, (rows, rows), 0)
    across = lax.broadcasted_iota(jnp.int32, (rows, rows), 1)
    allowed = image_plan(info, down, images, 1)[0] == image_plan(info, across, images, 1)[0]
    for head in range(width // HD):
        columns = slice(head * HD, (head + 1) * HD)
        scores = lax.dot_general(
            query_ref[:, columns], key_ref[:, columns], (((1,), (1,)), ((), ())),
            preferred_element_type=jnp.float32,
        ) * (HD ** (-0.5))
        scores = jnp.where(allowed, scores, -1000000000.0)
        weights = jnp.exp(scores - jnp.max(scores, axis=-1, keepdims=True))
        weights_ref[head] = weights / jnp.sum(weights, axis=-1, keepdims=True)


def value_kernel(images, info, slots_ref, weights_ref, cot_ref, value_ref):
    slots, width = slots_ref.shape
    rows = cot_ref.shape[0]
    row = lax.broadcasted_iota(jnp.int32, (rows, slots), 0)
    _, position = image_plan(info, row, images, slots // images)
    pick = position == lax.broadcasted_iota(jnp.int32, (rows, slots), 1)
    pick = jnp.where(pick, 1.0, 0.0).astype(jnp.bfloat16)
    cot_ref[...] = jnp.dot(
        pick, slots_ref[...], preferred_element_type=jnp.float32
    ).astype(jnp.bfloat16)
    for head in range(width // HD):
        columns = slice(head * HD, (head + 1) * HD)
        value_ref[:, columns] = lax.dot_general(
            weights_ref[head].astype(jnp.bfloat16), cot_ref[:, columns], (((0,), (0,)), ((), ())),
            preferred_element_type=jnp.float32,
        ).astype(jnp.bfloat16)


def spread_of(values):
    mean = jnp.sum(values, axis=-1, keepdims=True) * (1.0 / values.shape[1])
    centred = values - mean
    return mean, jnp.sum(centred * centred, axis=-1, keepdims=True)


def stats_kernel(own, one, two, stats_ref):
    rows = own.shape[0]
    lane = lax.broadcasted_iota(jnp.int32, (rows, 128), 1)
    table = jnp.zeros((rows, 128), jnp.float32)
    for index, ref in enumerate((own, one, two)):
        mean, spread = spread_of(ref[...].astype(jnp.float32))
        table = jnp.where(lane == index, mean, table)
        table = jnp.where(lane == index + 3, spread, table)
    stats_ref[...] = table


def norm_kernel(info, stats_ref, gain_ref, own, one, two, near, far, *rest):
    values, outs, (packed_ref, source, sems) = rest[:4], rest[4:12], rest[12:]
    device, layer = 2 * info[0] + info[1], info[2]
    outer = (layer == 0) | (layer == 3)
    rows, half = outs[0].shape

    def copy(index, ref):
        return pltpu.make_async_copy(ref, source.at[index], sems.at[index])

    @pl.when(outer)
    def _():
        copy(3, far).start()

    @pl.when(jnp.logical_not(outer))
    def _():
        copy(3, near).start()

    for index, ref in enumerate((own, one, two)):
        copy(index, ref).start()
    for index, ref in enumerate(values):
        packed_ref[index] = ref[...]
    copy(3, far).wait()
    columns = 8 * half
    last_mean, last_spread = spread_of(source[3].astype(jnp.float32))
    table = stats_ref[...]
    means = [table[:, index:index + 1] for index in range(3)] + [last_mean]
    mean = sum(means) * 0.25
    shift = sum((part - mean) * (part - mean) for part in means) * (2 * half)
    spread = table[:, 3:4] + table[:, 4:5] + table[:, 5:6] + last_spread + shift
    rstd = lax.rsqrt(spread * (1.0 / columns) + 1e-06)
    for index, ref in enumerate((own, one, two)):
        copy(index, ref).wait()

    for offset, out in enumerate(outs):
        block = device ^ offset
        start = pl.multiple_of((block % 2) * half, half)
        values = source[(block // 2) ^ layer, :, pl.ds(start, half)]
        gain = gain_ref[pl.ds(block, 1), :]
        out[...] = ((values.astype(jnp.float32) - mean) * rstd * gain).astype(jnp.bfloat16)


def backward_kernel(info, weight_ref, query_ref, key_ref, cot_ref, weights_ref, *refs):
    normed, (query_out, key_out, total) = refs[:8], refs[8:]
    device = 2 * info[0] + info[1]
    half = normed[0].shape[1]
    for offset, ref in enumerate(normed):
        start = pl.multiple_of((device ^ offset) * half, half)
        part = jnp.dot(ref[...], weight_ref[pl.ds(start, half), :], preferred_element_type=jnp.float32)
        total[...] = total[...] + part if offset else part
    scale = HD ** (-0.5)
    for head in range(query_ref.shape[1] // HD):
        columns = slice(head * HD, (head + 1) * HD)
        weights = weights_ref[head]
        prob_grad = lax.dot_general(
            cot_ref[:, columns], total[:, columns].astype(jnp.bfloat16), (((1,), (1,)), ((), ())),
            preferred_element_type=jnp.float32,
        )
        centre = jnp.sum(weights * prob_grad, axis=-1, keepdims=True)
        score_grad = (weights * (prob_grad - centre)).astype(jnp.bfloat16)
        query_out[:, columns] = (
            jnp.dot(score_grad, key_ref[:, columns], preferred_element_type=jnp.float32) * scale
        ).astype(jnp.bfloat16)
        key_out[:, columns] = (
            lax.dot_general(
                score_grad, query_ref[:, columns], (((0,), (0,)), ((), ())),
                preferred_element_type=jnp.float32,
            ) * scale
        ).astype(jnp.bfloat16)


def joined(offsets, normed, chip_values, mate_values):
    right = [mate_values[offset // 2] if offset % 2 else chip_values[offset // 2][...] for offset in offsets]
    return jnp.concatenate([ref[...] for ref in normed], axis=0), jnp.concatenate(right, axis=0)


def gradient_first_kernel(offsets, *refs):
    count = len(offsets)
    left, right = joined(offsets, refs[:count], refs[count:count + 4], refs[count + 4])
    refs[count + 5][...] = lax.dot_general(
        left, right, (((0,), (0,)), ((), ())), preferred_element_type=jnp.float32
    )


def gradient_last_kernel(offsets, before, *refs):
    count = len(offsets)
    left, right = joined(offsets, refs[:count], refs[count:count + 4], refs[count + 4])
    out_ref, ready, done = refs[count + 5:]
    blocks, _, columns = ready.shape
    copies = []
    for block in range(blocks):
        part = slice(block * columns, (block + 1) * columns)
        ready[block] = before[:, part] + lax.dot_general(
            left, right[:, part], (((0,), (0,)), ((), ())), preferred_element_type=jnp.float32
        )
        copies.append(
            pltpu.make_async_copy(ready.at[block], out_ref.at[:, pl.ds(block * columns, columns)], done.at[block])
        )
        copies[-1].start()
    for copy in copies:
        copy.wait()


def shape(dims, dtype=jnp.bfloat16):
    return jax.ShapeDtypeStruct(dims, dtype)


VMEM_LIMIT = 24 * 1024 * 1024
BIG = 56 * 1024 * 1024
SMEM = pl.BlockSpec(memory_space=pltpu.SMEM)
WHOLE = pl.BlockSpec(memory_space=pltpu.VMEM)
ANY = pl.BlockSpec(memory_space=pl.ANY)


def call(kernel, name, out_shape, in_specs, out_specs, scratch=(), limit=VMEM_LIMIT, after=()):
    used = len(in_specs)

    def body(*refs):
        return kernel(*refs[:used], *refs[used + len(after):])

    made = pl.pallas_call(
        body,
        name=name,
        out_shape=out_shape,
        in_specs=list(in_specs) + [ANY] * len(after),
        out_specs=out_specs,
        scratch_shapes=list(scratch),
        cost_estimate=pl.CostEstimate(flops=1, bytes_accessed=1, transcendentals=0),
        compiler_params=pltpu.CompilerParams(vmem_limit_bytes=limit),
    )
    return lambda *args: made(*args, *after)


def across(rows, distance):
    return lax.ppermute(rows, "dp", [(i, i ^ distance) for i in range(8)])


def between_chips(blocks):
    return lax.all_to_all(
        blocks, "dp", split_axis=0, concat_axis=0, tiled=True,
        axis_index_groups=[[0, 2, 4, 6], [1, 3, 5, 7]],
    )


def fast_body(
    patches, norm_gain, value_weight, queries, key_vectors, head_cotangent, image_owner, patch_count
):
    rows, columns = patches.shape
    half = columns // 2
    width = queries.shape[1]
    heads = width // HD
    images = image_owner.shape[1]
    slots = head_cotangent.shape[0]
    device = lax.axis_index("dp").astype(jnp.int32)
    place = [device // 2, device % 2, lax.axis_index("mp").astype(jnp.int32)]
    info = jnp.concatenate([
        jnp.stack(place + [jnp.int32(0)] * (HEADER - 3)),
        lax.dynamic_index_in_dim(image_owner, device, 0, keepdims=False),
        lax.dynamic_index_in_dim(patch_count, device, 0, keepdims=False),
    ])
    flat = (rows, width)

    received = lax.all_to_all(
        head_cotangent.reshape(8, slots // 8, width), "dp", split_axis=0, concat_axis=0, tiled=True
    ).reshape(slots, width)
    two = lax.ppermute(patches, "mp", [(0, 2), (2, 0), (1, 3), (3, 1)])
    one = lax.ppermute(patches, "mp", [(0, 1), (1, 0), (2, 3), (3, 2)])

    weights, gain = call(
        functools.partial(weights_kernel, images), "attention_weights",
        (shape((heads, rows, rows), jnp.float32), shape((8, half), jnp.float32)), [SMEM] + [WHOLE] * 3, (WHOLE, WHOLE),
    )(info, norm_gain.reshape(8, half), queries, key_vectors)
    cotangent, value_rows = call(
        functools.partial(value_kernel, images), "value_rows",
        (shape(flat), shape(flat)), [SMEM, WHOLE, WHOLE], (WHOLE, WHOLE),
    )(info, received, weights)
    middle, passed, first_one, _ = lax.optimization_barrier((patches, two, one, value_rows))
    near = lax.ppermute(middle, "mp", [(1, 2), (2, 1)])
    far = lax.ppermute(passed, "mp", [(2, 3), (1, 0)])
    chip_values = [value_rows] + [across(value_rows, distance) for distance in (2, 4, 6)]

    block = shape((rows, half))
    stats = call(
        stats_kernel, "partial_stats", shape((rows, 128), jnp.float32), [WHOLE] * 3, WHOLE,
    )(middle, first_one, passed)
    *normed, packed = call(
        norm_kernel, "norm_rows", (block,) * 8 + (shape((4,) + flat),),
        [SMEM, WHOLE, WHOLE] + [ANY] * 5 + [WHOLE] * 4, (WHOLE,) * 9,
        (pltpu.VMEM((4, rows, columns), jnp.bfloat16), pltpu.SemaphoreType.DMA((4,))),
    )(info, stats, gain, patches, one, two, near, far, *chip_values)

    query_grad, key_grad = call(
        backward_kernel, "attention_backward", (shape(flat), shape(flat)),
        [SMEM] + [WHOLE] * 13, (WHOLE,) * 2, (pltpu.VMEM(flat, jnp.float32),),
    )(info, value_weight, queries, key_vectors, cotangent, weights, *normed)
    mate_values = across(packed, 1)

    held = lax.optimization_barrier([normed[offset] for offset in LATE] + [query_grad])
    sent = list(normed)
    for offset, part in zip(LATE, held):
        sent[offset] = part
    moved = [sent[0]] + [across(sent[offset], offset) for offset in range(1, 8)]
    early = [offset for offset in range(8) if offset not in LATE]
    late = [offset for offset in range(8) if offset not in early]

    grad = shape((half, width), jnp.float32)
    partial = call(
        functools.partial(gradient_first_kernel, early), "gradient_first", grad, [WHOLE] * (len(early) + 5), WHOLE
    )(*[moved[offset] for offset in early], *chip_values, mate_values)
    blocks = width // 256
    weight_grad = call(
        functools.partial(gradient_last_kernel, late), "gradient_last", grad, [WHOLE] * (len(late) + 6), ANY,
        (pltpu.VMEM((blocks, half, 256), jnp.float32), pltpu.SemaphoreType.DMA((blocks,))),
        after=(query_grad,),
    )(partial, *[moved[offset] for offset in late], *chip_values, mate_values)
    return weight_grad, query_grad, key_grad


def solution(mesh):
    fast = mesh.shape["dp"] == 8 and mesh.shape["mp"] == 4
    return jax.shard_map(
        fast_body if fast else general_body,
        mesh=mesh,
        in_specs=(
            P("dp", "mp"),
            P(),
            P(None, "mp"),
            P("dp", "mp"),
            P("dp", "mp"),
            P("dp", "mp"),
            P(),
            P(),
        ),
        out_specs=(P("dp", "mp"), P("dp", "mp"), P("dp", "mp")),
        check_vma=False,
    )
```

```python
import functools

import jax
import jax.numpy as jnp
from jax import lax
from jax.experimental import pallas as pl
from jax.experimental.pallas import tpu as pltpu
from jax.sharding import PartitionSpec as P

HD = 128
HEADER = 8
LATE = (3,5)


def normalize(rows, norm_gain):
    values = rows.astype(jnp.float32)
    average = jnp.mean(values, axis=-1, keepdims=True)
    centred = values - average
    variance = jnp.mean(centred * centred, axis=-1, keepdims=True)
    return (centred * lax.rsqrt(variance + 1e-06) * norm_gain).astype(jnp.bfloat16)


def row_plan(image_owner, patch_count, rows_here, capacity, devices):
    device = lax.axis_index("dp")
    own_list = lax.dynamic_index_in_dim(image_owner, device, 0, keepdims=False)
    own_count = lax.dynamic_index_in_dim(patch_count, device, 0, keepdims=False)
    ends = jnp.cumsum(own_count)
    starts = ends - own_count
    row_index = jnp.arange(rows_here, dtype=jnp.int32)
    image_of = jnp.sum((ends[None, :] <= row_index[:, None]).astype(jnp.int32), axis=1)
    picked = image_of[:, None] == jnp.arange(devices, dtype=jnp.int32)[None, :]
    row_owner = jnp.sum(jnp.where(picked, own_list[None, :], 0), axis=1)
    row_start = jnp.sum(jnp.where(picked, starts[None, :], 0), axis=1)
    return image_of, row_owner * capacity + row_index - row_start


def attention_grads(query_rows, key_rows, value_rows, cotangent, segment):
    total, width = query_rows.shape
    heads = width // HD
    scale = HD ** (-0.5)

    def split(rows):
        return rows.reshape(total, heads, HD)

    query, key, value, cot = split(query_rows), split(key_rows), split(value_rows), split(cotangent)
    scores = jnp.einsum("qhd,khd->hqk", query, key, preferred_element_type=jnp.float32) * scale
    allowed = segment[:, None] == segment[None, :]
    scores = jnp.where(allowed[None], scores, -1000000000.0)
    weights = jnp.exp(scores - jnp.max(scores, axis=-1, keepdims=True))
    weights = weights / jnp.sum(weights, axis=-1, keepdims=True)
    value_grad = jnp.einsum(
        "hqk,qhd->khd", weights.astype(jnp.bfloat16), cot, preferred_element_type=jnp.float32
    )
    prob_grad = jnp.einsum("qhd,khd->hqk", cot, value, preferred_element_type=jnp.float32)
    centre = jnp.sum(weights * prob_grad, axis=-1, keepdims=True)
    score_grad = (weights * (prob_grad - centre)).astype(jnp.bfloat16)
    query_grad = jnp.einsum("hqk,khd->qhd", score_grad, key, preferred_element_type=jnp.float32)
    key_grad = jnp.einsum("hqk,qhd->khd", score_grad, query, preferred_element_type=jnp.float32)

    def join(rows):
        return rows.astype(jnp.bfloat16).reshape(total, width)

    return join(value_grad), join(query_grad * scale), join(key_grad * scale)


def general_body(
    patches, norm_gain, value_weight, queries, key_vectors, head_cotangent, image_owner, patch_count
):
    devices = lax.axis_size("dp")
    rows_here = patches.shape[0]
    width = queries.shape[1]
    capacity = head_cotangent.shape[0] // devices
    segment, index = row_plan(image_owner, patch_count, rows_here, capacity, devices)
    slots = lax.all_to_all(
        head_cotangent.reshape(devices, capacity, width), "dp", split_axis=0, concat_axis=0, tiled=True
    )
    cotangent = slots.reshape(devices * capacity, width)[index]
    normed = normalize(lax.all_gather(patches, "mp", axis=1, tiled=True), norm_gain)
    values = jnp.dot(normed, value_weight, preferred_element_type=jnp.float32).astype(jnp.bfloat16)
    value_rows, query_grad, key_grad = attention_grads(
        queries, key_vectors, values, cotangent, segment
    )
    all_value_rows = lax.all_gather(value_rows, "dp", axis=0, tiled=True)
    columns = jnp.swapaxes(normed.reshape(rows_here, devices, -1), 0, 1)
    columns = lax.all_to_all(columns, "dp", split_axis=0, concat_axis=0, tiled=True)
    columns = columns.reshape(devices * rows_here, -1)
    weight_grad = lax.dot_general(
        columns, all_value_rows, (((0,), (0,)), ((), ())), preferred_element_type=jnp.float32
    )
    return weight_grad, query_grad, key_grad


def image_plan(info, row, images, capacity):
    image = jnp.zeros(row.shape, jnp.int32)
    position = jnp.zeros(row.shape, jnp.int32)
    start = jnp.int32(0)
    for index in range(images):
        end = start + info[HEADER + images + index]
        inside = (row >= start) & (row < end)
        image = jnp.where(inside, index, image)
        position = jnp.where(inside, info[HEADER + index] * capacity + row - start, position)
        start = end
    return image, position


def weights_kernel(images, info, gain_in, query_ref, key_ref, weights_ref, gain_ref):
    gain_ref[...] = gain_in[...]
    rows, width = query_ref.shape
    down = lax.broadcasted_iota(jnp.int32, (rows, rows), 0)
    across = lax.broadcasted_iota(jnp.int32, (rows, rows), 1)
    allowed = image_plan(info, down, images, 1)[0] == image_plan(info, across, images, 1)[0]
    for head in range(width // HD):
        columns = slice(head * HD, (head + 1) * HD)
        scores = lax.dot_general(
            query_ref[:, columns], key_ref[:, columns], (((1,), (1,)), ((), ())),
            preferred_element_type=jnp.float32,
        ) * (HD ** (-0.5))
        scores = jnp.where(allowed, scores, -1000000000.0)
        weights = jnp.exp(scores - jnp.max(scores, axis=-1, keepdims=True))
        weights_ref[head] = weights / jnp.sum(weights, axis=-1, keepdims=True)


def value_kernel(images, info, slots_ref, weights_ref, cot_ref, value_ref):
    slots, width = slots_ref.shape
    rows = cot_ref.shape[0]
    row = lax.broadcasted_iota(jnp.int32, (rows, slots), 0)
    _, position = image_plan(info, row, images, slots // images)
    pick = position == lax.broadcasted_iota(jnp.int32, (rows, slots), 1)
    pick = jnp.where(pick, 1.0, 0.0).astype(jnp.bfloat16)
    cot_ref[...] = jnp.dot(
        pick, slots_ref[...], preferred_element_type=jnp.float32
    ).astype(jnp.bfloat16)
    for head in range(width // HD):
        columns = slice(head * HD, (head + 1) * HD)
        value_ref[:, columns] = lax.dot_general(
            weights_ref[head].astype(jnp.bfloat16), cot_ref[:, columns], (((0,), (0,)), ((), ())),
            preferred_element_type=jnp.float32,
        ).astype(jnp.bfloat16)


def spread_of(values):
    mean = jnp.sum(values, axis=-1, keepdims=True) * (1.0 / values.shape[1])
    centred = values - mean
    return mean, jnp.sum(centred * centred, axis=-1, keepdims=True)


def stats_kernel(own, one, two, stats_ref):
    rows = own.shape[0]
    lane = lax.broadcasted_iota(jnp.int32, (rows, 128), 1)
    table = jnp.zeros((rows, 128), jnp.float32)
    for index, ref in enumerate((own, one, two)):
        mean, spread = spread_of(ref[...].astype(jnp.float32))
        table = jnp.where(lane == index, mean, table)
        table = jnp.where(lane == index + 3, spread, table)
    stats_ref[...] = table


def norm_kernel(info, stats_ref, gain_ref, own, one, two, near, far, *rest):
    values, outs, (packed_ref, source, sems) = rest[:4], rest[4:12], rest[12:]
    device, layer = 2 * info[0] + info[1], info[2]
    outer = (layer == 0) | (layer == 3)
    rows, half = outs[0].shape

    def copy(index, ref):
        return pltpu.make_async_copy(ref, source.at[index], sems.at[index])

    @pl.when(outer)
    def _():
        copy(3, far).start()

    @pl.when(jnp.logical_not(outer))
    def _():
        copy(3, near).start()

    for index, ref in enumerate((own, one, two)):
        copy(index, ref).start()
    for index, ref in enumerate(values):
        packed_ref[index] = ref[...]
    copy(3, far).wait()
    columns = 8 * half
    last_mean, last_spread = spread_of(source[3].astype(jnp.float32))
    table = stats_ref[...]
    means = [table[:, index:index + 1] for index in range(3)] + [last_mean]
    mean = sum(means) * 0.25
    shift = sum((part - mean) * (part - mean) for part in means) * (2 * half)
    spread = table[:, 3:4] + table[:, 4:5] + table[:, 5:6] + last_spread + shift
    rstd = lax.rsqrt(spread * (1.0 / columns) + 1e-06)
    for index, ref in enumerate((own, one, two)):
        copy(index, ref).wait()

    for offset, out in enumerate(outs):
        block = device ^ offset
        start = pl.multiple_of((block % 2) * half, half)
        values = source[(block // 2) ^ layer, :, pl.ds(start, half)]
        gain = gain_ref[pl.ds(block, 1), :]
        out[...] = ((values.astype(jnp.float32) - mean) * rstd * gain).astype(jnp.bfloat16)


def backward_kernel(info, weight_ref, query_ref, key_ref, cot_ref, weights_ref, *refs):
    normed, (query_out, key_out, total) = refs[:8], refs[8:]
    device = 2 * info[0] + info[1]
    half = normed[0].shape[1]
    for offset, ref in enumerate(normed):
        start = pl.multiple_of((device ^ offset) * half, half)
        part = jnp.dot(ref[...], weight_ref[pl.ds(start, half), :], preferred_element_type=jnp.float32)
        total[...] = total[...] + part if offset else part
    scale = HD ** (-0.5)
    for head in range(query_ref.shape[1] // HD):
        columns = slice(head * HD, (head + 1) * HD)
        weights = weights_ref[head]
        prob_grad = lax.dot_general(
            cot_ref[:, columns], total[:, columns].astype(jnp.bfloat16), (((1,), (1,)), ((), ())),
            preferred_element_type=jnp.float32,
        )
        centre = jnp.sum(weights * prob_grad, axis=-1, keepdims=True)
        score_grad = (weights * (prob_grad - centre)).astype(jnp.bfloat16)
        query_out[:, columns] = (
            jnp.dot(score_grad, key_ref[:, columns], preferred_element_type=jnp.float32) * scale
        ).astype(jnp.bfloat16)
        key_out[:, columns] = (
            lax.dot_general(
                score_grad, query_ref[:, columns], (((0,), (0,)), ((), ())),
                preferred_element_type=jnp.float32,
            ) * scale
        ).astype(jnp.bfloat16)


def joined(offsets, normed, chip_values, mate_values):
    right = [mate_values[offset // 2] if offset % 2 else chip_values[offset // 2][...] for offset in offsets]
    return jnp.concatenate([ref[...] for ref in normed], axis=0), jnp.concatenate(right, axis=0)


def gradient_first_kernel(offsets, *refs):
    count = len(offsets)
    left, right = joined(offsets, refs[:count], refs[count:count + 4], refs[count + 4])
    refs[count + 5][...] = lax.dot_general(
        left, right, (((0,), (0,)), ((), ())), preferred_element_type=jnp.float32
    )


def gradient_last_kernel(offsets, before, *refs):
    count = len(offsets)
    left, right = joined(offsets, refs[:count], refs[count:count + 4], refs[count + 4])
    out_ref, ready, done = refs[count + 5:]
    blocks, _, columns = ready.shape
    copies = []
    for block in range(blocks):
        part = slice(block * columns, (block + 1) * columns)
        ready[block] = before[:, part] + lax.dot_general(
            left, right[:, part], (((0,), (0,)), ((), ())), preferred_element_type=jnp.float32
        )
        copies.append(
            pltpu.make_async_copy(ready.at[block], out_ref.at[:, pl.ds(block * columns, columns)], done.at[block])
        )
        copies[-1].start()
    for copy in copies:
        copy.wait()


def shape(dims, dtype=jnp.bfloat16):
    return jax.ShapeDtypeStruct(dims, dtype)


VMEM_LIMIT = 24 * 1024 * 1024
BIG = 56 * 1024 * 1024
SMEM = pl.BlockSpec(memory_space=pltpu.SMEM)
WHOLE = pl.BlockSpec(memory_space=pltpu.VMEM)
ANY = pl.BlockSpec(memory_space=pl.ANY)


def call(kernel, name, out_shape, in_specs, out_specs, scratch=(), limit=VMEM_LIMIT, after=()):
    used = len(in_specs)

    def body(*refs):
        return kernel(*refs[:used], *refs[used + len(after):])

    made = pl.pallas_call(
        body,
        name=name,
        out_shape=out_shape,
        in_specs=list(in_specs) + [ANY] * len(after),
        out_specs=out_specs,
        scratch_shapes=list(scratch),
        cost_estimate=pl.CostEstimate(flops=1, bytes_accessed=1, transcendentals=0),
        compiler_params=pltpu.CompilerParams(vmem_limit_bytes=limit),
    )
    return lambda *args: made(*args, *after)


def across(rows, distance):
    return lax.ppermute(rows, "dp", [(i, i ^ distance) for i in range(8)])


def between_chips(blocks):
    return lax.all_to_all(
        blocks, "dp", split_axis=0, concat_axis=0, tiled=True,
        axis_index_groups=[[0, 2, 4, 6], [1, 3, 5, 7]],
    )


def fast_body(
    patches, norm_gain, value_weight, queries, key_vectors, head_cotangent, image_owner, patch_count
):
    rows, columns = patches.shape
    half = columns // 2
    width = queries.shape[1]
    heads = width // HD
    images = image_owner.shape[1]
    slots = head_cotangent.shape[0]
    device = lax.axis_index("dp").astype(jnp.int32)
    place = [device // 2, device % 2, lax.axis_index("mp").astype(jnp.int32)]
    info = jnp.concatenate([
        jnp.stack(place + [jnp.int32(0)] * (HEADER - 3)),
        lax.dynamic_index_in_dim(image_owner, device, 0, keepdims=False),
        lax.dynamic_index_in_dim(patch_count, device, 0, keepdims=False),
    ])
    flat = (rows, width)

    received = lax.all_to_all(
        head_cotangent.reshape(8, slots // 8, width), "dp", split_axis=0, concat_axis=0, tiled=True
    ).reshape(slots, width)
    two = lax.ppermute(patches, "mp", [(0, 2), (2, 0), (1, 3), (3, 1)])
    one = lax.ppermute(patches, "mp", [(0, 1), (1, 0), (2, 3), (3, 2)])

    weights, gain = call(
        functools.partial(weights_kernel, images), "attention_weights",
        (shape((heads, rows, rows), jnp.float32), shape((8, half), jnp.float32)), [SMEM] + [WHOLE] * 3, (WHOLE, WHOLE),
    )(info, norm_gain.reshape(8, half), queries, key_vectors)
    cotangent, value_rows = call(
        functools.partial(value_kernel, images), "value_rows",
        (shape(flat), shape(flat)), [SMEM, WHOLE, WHOLE], (WHOLE, WHOLE),
    )(info, received, weights)
    middle, passed, first_one, _ = lax.optimization_barrier((patches, two, one, value_rows))
    near = lax.ppermute(middle, "mp", [(1, 2), (2, 1)])
    far = lax.ppermute(passed, "mp", [(2, 3), (1, 0)])
    chip_values = [value_rows] + [across(value_rows, distance) for distance in (2, 4, 6)]

    block = shape((rows, half))
    stats = call(
        stats_kernel, "partial_stats", shape((rows, 128), jnp.float32), [WHOLE] * 3, WHOLE, after=(value_weight,),
    )(middle, first_one, passed)
    *normed, packed = call(
        norm_kernel, "norm_rows", (block,) * 8 + (shape((4,) + flat),),
        [SMEM, WHOLE, WHOLE] + [ANY] * 5 + [WHOLE] * 4, (WHOLE,) * 9,
        (pltpu.VMEM((4, rows, columns), jnp.bfloat16), pltpu.SemaphoreType.DMA((4,))),
    )(info, stats, gain, patches, one, two, near, far, *chip_values)

    mate_values = across(packed, 1)
    mate_rows = across(normed[1], 1)
    query_grad, key_grad = call(
        backward_kernel, "attention_backward", (shape(flat), shape(flat)),
        [SMEM] + [WHOLE] * 13, (WHOLE,) * 2, (pltpu.VMEM(flat, jnp.float32),),
        after=(mate_values, mate_rows),
    )(info, value_weight, queries, key_vectors, cotangent, weights, *normed)

    held = lax.optimization_barrier([normed[offset] for offset in LATE] + [query_grad])
    sent = list(normed)
    for offset, part in zip(LATE, held):
        sent[offset] = part
    moved = [sent[0], mate_rows] + [across(sent[offset], offset) for offset in range(2, 8)]
    early = [offset for offset in range(8) if offset not in LATE]
    late = [offset for offset in range(8) if offset not in early]

    grad = shape((half, width), jnp.float32)
    partial = call(
        functools.partial(gradient_first_kernel, early), "gradient_first", grad, [WHOLE] * (len(early) + 5), WHOLE
    )(*[moved[offset] for offset in early], *chip_values, mate_values)
    blocks = width // 256
    weight_grad = call(
        functools.partial(gradient_last_kernel, late), "gradient_last", grad, [WHOLE] * (len(late) + 6), ANY,
        (pltpu.VMEM((blocks, half, 256), jnp.float32), pltpu.SemaphoreType.DMA((blocks,))),
        after=(query_grad,),
    )(partial, *[moved[offset] for offset in late], *chip_values, mate_values)
    return weight_grad, query_grad, key_grad


def solution(mesh):
    fast = mesh.shape["dp"] == 8 and mesh.shape["mp"] == 4
    return jax.shard_map(
        fast_body if fast else general_body,
        mesh=mesh,
        in_specs=(
            P("dp", "mp"),
            P(),
            P(None, "mp"),
            P("dp", "mp"),
            P("dp", "mp"),
            P("dp", "mp"),
            P(),
            P(),
        ),
        out_specs=(P("dp", "mp"), P("dp", "mp"), P("dp", "mp")),
        check_vma=False,
    )
```

```python
import functools

import jax
import jax.numpy as jnp
from jax import lax
from jax.experimental import pallas as pl
from jax.experimental.pallas import tpu as pltpu
from jax.sharding import PartitionSpec as P

HD = 128
HEADER = 8
FIRST = (0,6,7,2,4,1)
LAST = (16,17,3,5)
LATE = (16,17,3,5)
HALVED = (6, 7)


def normalize(rows, norm_gain):
    values = rows.astype(jnp.float32)
    average = jnp.mean(values, axis=-1, keepdims=True)
    centred = values - average
    variance = jnp.mean(centred * centred, axis=-1, keepdims=True)
    return (centred * lax.rsqrt(variance + 1e-06) * norm_gain).astype(jnp.bfloat16)


def row_plan(image_owner, patch_count, rows_here, capacity, devices):
    device = lax.axis_index("dp")
    own_list = lax.dynamic_index_in_dim(image_owner, device, 0, keepdims=False)
    own_count = lax.dynamic_index_in_dim(patch_count, device, 0, keepdims=False)
    ends = jnp.cumsum(own_count)
    starts = ends - own_count
    row_index = jnp.arange(rows_here, dtype=jnp.int32)
    image_of = jnp.sum((ends[None, :] <= row_index[:, None]).astype(jnp.int32), axis=1)
    picked = image_of[:, None] == jnp.arange(devices, dtype=jnp.int32)[None, :]
    row_owner = jnp.sum(jnp.where(picked, own_list[None, :], 0), axis=1)
    row_start = jnp.sum(jnp.where(picked, starts[None, :], 0), axis=1)
    return image_of, row_owner * capacity + row_index - row_start


def attention_grads(query_rows, key_rows, value_rows, cotangent, segment):
    total, width = query_rows.shape
    heads = width // HD
    scale = HD ** (-0.5)

    def split(rows):
        return rows.reshape(total, heads, HD)

    query, key, value, cot = split(query_rows), split(key_rows), split(value_rows), split(cotangent)
    scores = jnp.einsum("qhd,khd->hqk", query, key, preferred_element_type=jnp.float32) * scale
    allowed = segment[:, None] == segment[None, :]
    scores = jnp.where(allowed[None], scores, -1000000000.0)
    weights = jnp.exp(scores - jnp.max(scores, axis=-1, keepdims=True))
    weights = weights / jnp.sum(weights, axis=-1, keepdims=True)
    value_grad = jnp.einsum(
        "hqk,qhd->khd", weights.astype(jnp.bfloat16), cot, preferred_element_type=jnp.float32
    )
    prob_grad = jnp.einsum("qhd,khd->hqk", cot, value, preferred_element_type=jnp.float32)
    centre = jnp.sum(weights * prob_grad, axis=-1, keepdims=True)
    score_grad = (weights * (prob_grad - centre)).astype(jnp.bfloat16)
    query_grad = jnp.einsum("hqk,khd->qhd", score_grad, key, preferred_element_type=jnp.float32)
    key_grad = jnp.einsum("hqk,qhd->khd", score_grad, query, preferred_element_type=jnp.float32)

    def join(rows):
        return rows.astype(jnp.bfloat16).reshape(total, width)

    return join(value_grad), join(query_grad * scale), join(key_grad * scale)


def general_body(
    patches, norm_gain, value_weight, queries, key_vectors, head_cotangent, image_owner, patch_count
):
    devices = lax.axis_size("dp")
    rows_here = patches.shape[0]
    width = queries.shape[1]
    capacity = head_cotangent.shape[0] // devices
    segment, index = row_plan(image_owner, patch_count, rows_here, capacity, devices)
    slots = lax.all_to_all(
        head_cotangent.reshape(devices, capacity, width), "dp", split_axis=0, concat_axis=0, tiled=True
    )
    cotangent = slots.reshape(devices * capacity, width)[index]
    normed = normalize(lax.all_gather(patches, "mp", axis=1, tiled=True), norm_gain)
    values = jnp.dot(normed, value_weight, preferred_element_type=jnp.float32).astype(jnp.bfloat16)
    value_rows, query_grad, key_grad = attention_grads(
        queries, key_vectors, values, cotangent, segment
    )
    all_value_rows = lax.all_gather(value_rows, "dp", axis=0, tiled=True)
    columns = jnp.swapaxes(normed.reshape(rows_here, devices, -1), 0, 1)
    columns = lax.all_to_all(columns, "dp", split_axis=0, concat_axis=0, tiled=True)
    columns = columns.reshape(devices * rows_here, -1)
    weight_grad = lax.dot_general(
        columns, all_value_rows, (((0,), (0,)), ((), ())), preferred_element_type=jnp.float32
    )
    return weight_grad, query_grad, key_grad


def image_plan(info, row, images, capacity):
    image = jnp.zeros(row.shape, jnp.int32)
    position = jnp.zeros(row.shape, jnp.int32)
    start = jnp.int32(0)
    for index in range(images):
        end = start + info[HEADER + images + index]
        inside = (row >= start) & (row < end)
        image = jnp.where(inside, index, image)
        position = jnp.where(inside, info[HEADER + index] * capacity + row - start, position)
        start = end
    return image, position


def weights_kernel(images, info, gain_in, query_ref, key_ref, weights_ref, gain_ref):
    gain_ref[...] = gain_in[...]
    rows, width = query_ref.shape
    down = lax.broadcasted_iota(jnp.int32, (rows, rows), 0)
    across = lax.broadcasted_iota(jnp.int32, (rows, rows), 1)
    allowed = image_plan(info, down, images, 1)[0] == image_plan(info, across, images, 1)[0]
    for head in range(width // HD):
        columns = slice(head * HD, (head + 1) * HD)
        scores = lax.dot_general(
            query_ref[:, columns], key_ref[:, columns], (((1,), (1,)), ((), ())),
            preferred_element_type=jnp.float32,
        ) * (HD ** (-0.5))
        scores = jnp.where(allowed, scores, -1000000000.0)
        weights = jnp.exp(scores - jnp.max(scores, axis=-1, keepdims=True))
        weights_ref[head] = weights / jnp.sum(weights, axis=-1, keepdims=True)


def value_kernel(images, info, slots_ref, weights_ref, cot_ref, value_ref):
    slots, width = slots_ref.shape
    rows = cot_ref.shape[0]
    row = lax.broadcasted_iota(jnp.int32, (rows, slots), 0)
    _, position = image_plan(info, row, images, slots // images)
    pick = position == lax.broadcasted_iota(jnp.int32, (rows, slots), 1)
    pick = jnp.where(pick, 1.0, 0.0).astype(jnp.bfloat16)
    cot_ref[...] = jnp.dot(
        pick, slots_ref[...], preferred_element_type=jnp.float32
    ).astype(jnp.bfloat16)
    for head in range(width // HD):
        columns = slice(head * HD, (head + 1) * HD)
        value_ref[:, columns] = lax.dot_general(
            weights_ref[head].astype(jnp.bfloat16), cot_ref[:, columns], (((0,), (0,)), ((), ())),
            preferred_element_type=jnp.float32,
        ).astype(jnp.bfloat16)


def spread_of(values):
    mean = jnp.sum(values, axis=-1, keepdims=True) * (1.0 / values.shape[1])
    centred = values - mean
    return mean, jnp.sum(centred * centred, axis=-1, keepdims=True)


def stats_kernel(info, own, one, two, stats_ref, arranged):
    for index, ref in enumerate((own, one, two)):
        arranged[index ^ info[2]] = ref[...]
    rows = own.shape[0]
    lane = lax.broadcasted_iota(jnp.int32, (rows, 128), 1)
    table = jnp.zeros((rows, 128), jnp.float32)
    for index, ref in enumerate((own, one, two)):
        mean, spread = spread_of(ref[...].astype(jnp.float32))
        table = jnp.where(lane == index, mean, table)
        table = jnp.where(lane == index + 3, spread, table)
    stats_ref[...] = table


def norm_kernel(info, stats_ref, gain_ref, arranged, near, far, *rest):
    outs, halves, last_ref = rest[:8], rest[8:-1], rest[-1]
    device, layer = 2 * info[0] + info[1], info[2]
    rows, half = outs[0].shape
    last = near[...].astype(jnp.float32) + far[...].astype(jnp.float32)
    last_ref[...] = last.astype(jnp.bfloat16)
    columns = 8 * half
    last_mean, last_spread = spread_of(last)
    table = stats_ref[...]
    means = [table[:, index:index + 1] for index in range(3)] + [last_mean]
    mean = sum(means) * 0.25
    shift = sum((part - mean) * (part - mean) for part in means) * (2 * half)
    spread = table[:, 3:4] + table[:, 4:5] + table[:, 5:6] + last_spread + shift
    rstd = lax.rsqrt(spread * (1.0 / columns) + 1e-06)
    for offset, out in enumerate(outs):
        block = device ^ offset
        start = pl.multiple_of((block % 2) * half, half)
        origin = block // 2
        values = jnp.where(
            (origin ^ layer) == 3, last_ref[:, pl.ds(start, half)], arranged[origin, :, pl.ds(start, half)]
        )
        gain = gain_ref[pl.ds(block, 1), :]
        out[...] = ((values.astype(jnp.float32) - mean) * rstd * gain).astype(jnp.bfloat16)
    first = pl.multiple_of((layer % 2) * (rows // 2), rows // 2)
    for offset, ref in zip(HALVED, halves):
        ref[...] = outs[offset][pl.ds(first, rows // 2), :]


def pack_kernel(*refs):
    for index, ref in enumerate(refs[:4]):
        refs[4][index] = ref[...]


def project_kernel(info, weight_ref, *refs):
    normed, (value_ref, total) = refs[:8], refs[8:]
    device = 2 * info[0] + info[1]
    half = normed[0].shape[1]
    for offset, ref in enumerate(normed):
        start = pl.multiple_of((device ^ offset) * half, half)
        part = jnp.dot(ref[...], weight_ref[pl.ds(start, half), :], preferred_element_type=jnp.float32)
        if offset == 0:
            total[...] = part
        elif offset < 7:
            total[...] += part
        else:
            value_ref[...] = (total[...] + part).astype(jnp.bfloat16)


def backward_kernel(value_ref, query_ref, key_ref, cot_ref, weights_ref, query_out, key_out):
    scale = HD ** (-0.5)
    for head in range(query_ref.shape[1] // HD):
        columns = slice(head * HD, (head + 1) * HD)
        weights = weights_ref[head]
        prob_grad = lax.dot_general(
            cot_ref[:, columns], value_ref[:, columns], (((1,), (1,)), ((), ())),
            preferred_element_type=jnp.float32,
        )
        centre = jnp.sum(weights * prob_grad, axis=-1, keepdims=True)
        score_grad = (weights * (prob_grad - centre)).astype(jnp.bfloat16)
        query_out[:, columns] = (
            jnp.dot(score_grad, key_ref[:, columns], preferred_element_type=jnp.float32) * scale
        ).astype(jnp.bfloat16)
        key_out[:, columns] = (
            lax.dot_general(
                score_grad, query_ref[:, columns], (((0,), (0,)), ((), ())),
                preferred_element_type=jnp.float32,
            ) * scale
        ).astype(jnp.bfloat16)


def joined(info, names, refs):
    refs = list(refs)
    chip_values, mate_values = refs[-5:-1], refs[-1]
    left, right = [], []
    for name in names:
        offset = name % 10
        values = mate_values.at[offset // 2] if offset % 2 else chip_values[offset // 2]
        left.append(refs.pop(0)[...])
        if offset in HALVED:
            rows = left[-1].shape[0]
            side = (info[2] + name // 10) % 2
            right.append(values[pl.ds(pl.multiple_of(side * rows, rows), rows), :])
        else:
            right.append(values[...])
    return jnp.concatenate(left, axis=0), jnp.concatenate(right, axis=0)


def gradient_first_kernel(names, info, *refs):
    left, right = joined(info, names, refs[:-1])
    refs[-1][...] = lax.dot_general(
        left, right, (((0,), (0,)), ((), ())), preferred_element_type=jnp.float32
    )


def gradient_last_kernel(names, info, before, *refs):
    left, right = joined(info, names, refs[:-3])
    out_ref, ready, done = refs[-3:]
    blocks, rows, _ = ready.shape
    copies = []
    for block in range(blocks):
        part = slice(block * rows, (block + 1) * rows)
        ready[block] = before[part, :] + lax.dot_general(
            left[:, part], right, (((0,), (0,)), ((), ())), preferred_element_type=jnp.float32
        )
        copies.append(
            pltpu.make_async_copy(ready.at[block], out_ref.at[pl.ds(block * rows, rows)], done.at[block])
        )
        copies[-1].start()
    for copy in copies:
        copy.wait()


def shape(dims, dtype=jnp.bfloat16):
    return jax.ShapeDtypeStruct(dims, dtype)


VMEM_LIMIT = 24 * 1024 * 1024
BIG = 56 * 1024 * 1024
SMEM = pl.BlockSpec(memory_space=pltpu.SMEM)
WHOLE = pl.BlockSpec(memory_space=pltpu.VMEM)
ANY = pl.BlockSpec(memory_space=pl.ANY)


def call(kernel, name, out_shape, in_specs, out_specs, scratch=(), limit=VMEM_LIMIT, after=()):
    used = len(in_specs)

    def body(*refs):
        return kernel(*refs[:used], *refs[used + len(after):])

    made = pl.pallas_call(
        body,
        name=name,
        out_shape=out_shape,
        in_specs=list(in_specs) + [ANY] * len(after),
        out_specs=out_specs,
        scratch_shapes=list(scratch),
        cost_estimate=pl.CostEstimate(flops=1, bytes_accessed=1, transcendentals=0),
        compiler_params=pltpu.CompilerParams(vmem_limit_bytes=limit),
    )
    return lambda *args: made(*args, *after)


def across(rows, distance):
    return lax.ppermute(rows, "dp", [(i, i ^ distance) for i in range(8)])


def between_chips(blocks):
    return lax.all_to_all(
        blocks, "dp", split_axis=0, concat_axis=0, tiled=True,
        axis_index_groups=[[0, 2, 4, 6], [1, 3, 5, 7]],
    )


def fast_body(
    patches, norm_gain, value_weight, queries, key_vectors, head_cotangent, image_owner, patch_count
):
    rows, columns = patches.shape
    half = columns // 2
    width = queries.shape[1]
    heads = width // HD
    images = image_owner.shape[1]
    slots = head_cotangent.shape[0]
    device = lax.axis_index("dp").astype(jnp.int32)
    place = [device // 2, device % 2, lax.axis_index("mp").astype(jnp.int32)]
    info = jnp.concatenate([
        jnp.stack(place + [jnp.int32(0)] * (HEADER - 3)),
        lax.dynamic_index_in_dim(image_owner, device, 0, keepdims=False),
        lax.dynamic_index_in_dim(patch_count, device, 0, keepdims=False),
    ])
    flat = (rows, width)

    received = lax.all_to_all(
        head_cotangent.reshape(8, slots // 8, width), "dp", split_axis=0, concat_axis=0, tiled=True
    ).reshape(slots, width)
    two = lax.ppermute(patches, "mp", [(0, 2), (2, 0), (1, 3), (3, 1)])
    one = lax.ppermute(patches, "mp", [(0, 1), (1, 0), (2, 3), (3, 2)])

    weights, gain = call(
        functools.partial(weights_kernel, images), "attention_weights",
        (shape((heads, rows, rows), jnp.float32), shape((8, half), jnp.float32)), [SMEM] + [WHOLE] * 3, (WHOLE, WHOLE),
    )(info, norm_gain.reshape(8, half), queries, key_vectors)
    cotangent, value_rows = call(
        functools.partial(value_kernel, images), "value_rows",
        (shape(flat), shape(flat)), [SMEM, WHOLE, WHOLE], (WHOLE, WHOLE),
    )(info, received, weights)
    middle, passed, first_one, _ = lax.optimization_barrier((patches, two, one, value_rows))
    near = lax.ppermute(middle, "mp", [(1, 2), (2, 1)])
    far = lax.ppermute(passed, "mp", [(2, 3), (1, 0)])
    chip_values = [value_rows] + [across(value_rows, distance) for distance in (2, 4, 6)]

    block = shape((rows, half))
    stats, arranged = call(
        stats_kernel, "partial_stats", (shape((rows, 128), jnp.float32), shape((4, rows, columns))),
        [SMEM] + [WHOLE] * 3, (WHOLE, WHOLE), after=(value_weight,),
    )(info, middle, first_one, passed)
    *normed, = call(
        norm_kernel, "norm_rows", (block,) * 8 + (shape((rows // 2, half)),) * len(HALVED),
        [SMEM] + [WHOLE] * 5, (WHOLE,) * (8 + len(HALVED)), (pltpu.VMEM((rows, columns), jnp.bfloat16),),
    )(info, stats, gain, arranged, near, far)
    normed, halves = normed[:8], normed[8:]
    packed = call(pack_kernel, "pack_values", shape((4,) + flat), [WHOLE] * 4, WHOLE, after=(normed[1],))(*chip_values)

    mate_values = across(packed, 1)
    mate_rows = across(normed[1], 1)
    values = call(
        project_kernel, "project_values", shape(flat), [SMEM] + [WHOLE] * 9, WHOLE, (pltpu.VMEM(flat, jnp.float32),),
        after=(mate_values, mate_rows),
    )(info, value_weight, *normed)
    query_grad, key_grad = call(
        backward_kernel, "attention_backward", (shape(flat), shape(flat)), [WHOLE] * 5, (WHOLE,) * 2,
    )(values, queries, key_vectors, cotangent, weights)

    moved = {0: normed[0], 1: mate_rows}
    sources = {offset: normed[offset] for offset in range(2, 8)} | dict(zip(HALVED, halves))
    for offset in range(2, 8):
        if offset not in LATE:
            moved[offset] = across(sources[offset], offset)
    held = [sources[name] if name < 10 else moved[name % 10] for name in LATE]
    held = lax.optimization_barrier(held + [values])
    for name, part in zip(LATE, held):
        if name < 10:
            moved[name] = across(part, name)
        else:
            moved[name] = lax.ppermute(part, "mp", [(0, 1), (1, 0), (2, 3), (3, 2)])
    for offset in HALVED:
        if offset + 10 not in moved:
            moved[offset + 10] = lax.ppermute(moved[offset], "mp", [(0, 1), (1, 0), (2, 3), (3, 2)])

    def arrived(names):
        return [moved[name] for name in names] + chip_values + [mate_values]

    grad = shape((half, width), jnp.float32)
    parts = arrived(FIRST)
    partial = call(
        functools.partial(gradient_first_kernel, FIRST), "gradient_first", grad, [SMEM] + [WHOLE] * len(parts), WHOLE
    )(info, *parts)
    parts = arrived(LAST)
    blocks = half // 256
    weight_grad = call(
        functools.partial(gradient_last_kernel, LAST), "gradient_last", grad, [SMEM] + [WHOLE] * (len(parts) + 1), ANY,
        (pltpu.VMEM((blocks, 256, width), jnp.float32), pltpu.SemaphoreType.DMA((blocks,))),
        after=(query_grad,),
    )(info, partial, *parts)
    return weight_grad, query_grad, key_grad


def solution(mesh):
    fast = mesh.shape["dp"] == 8 and mesh.shape["mp"] == 4
    return jax.shard_map(
        fast_body if fast else general_body,
        mesh=mesh,
        in_specs=(
            P("dp", "mp"),
            P(),
            P(None, "mp"),
            P("dp", "mp"),
            P("dp", "mp"),
            P("dp", "mp"),
            P(),
            P(),
        ),
        out_specs=(P("dp", "mp"), P("dp", "mp"), P("dp", "mp")),
        check_vma=False,
    )
```

```python
import functools

import jax
import jax.numpy as jnp
from jax import lax
from jax.experimental import pallas as pl
from jax.experimental.pallas import tpu as pltpu
from jax.sharding import PartitionSpec as P

HD = 128
HEADER = 8
FIRST = (0,6,7,2,4,1)
LAST = (20,3,5)
LATE = (20,3,5)
HALVED = (6, 7)
SWAPPED = 20


def normalize(rows, norm_gain):
    values = rows.astype(jnp.float32)
    average = jnp.mean(values, axis=-1, keepdims=True)
    centred = values - average
    variance = jnp.mean(centred * centred, axis=-1, keepdims=True)
    return (centred * lax.rsqrt(variance + 1e-06) * norm_gain).astype(jnp.bfloat16)


def row_plan(image_owner, patch_count, rows_here, capacity, devices):
    device = lax.axis_index("dp")
    own_list = lax.dynamic_index_in_dim(image_owner, device, 0, keepdims=False)
    own_count = lax.dynamic_index_in_dim(patch_count, device, 0, keepdims=False)
    ends = jnp.cumsum(own_count)
    starts = ends - own_count
    row_index = jnp.arange(rows_here, dtype=jnp.int32)
    image_of = jnp.sum((ends[None, :] <= row_index[:, None]).astype(jnp.int32), axis=1)
    picked = image_of[:, None] == jnp.arange(devices, dtype=jnp.int32)[None, :]
    row_owner = jnp.sum(jnp.where(picked, own_list[None, :], 0), axis=1)
    row_start = jnp.sum(jnp.where(picked, starts[None, :], 0), axis=1)
    return image_of, row_owner * capacity + row_index - row_start


def attention_grads(query_rows, key_rows, value_rows, cotangent, segment):
    total, width = query_rows.shape
    heads = width // HD
    scale = HD ** (-0.5)

    def split(rows):
        return rows.reshape(total, heads, HD)

    query, key, value, cot = split(query_rows), split(key_rows), split(value_rows), split(cotangent)
    scores = jnp.einsum("qhd,khd->hqk", query, key, preferred_element_type=jnp.float32) * scale
    allowed = segment[:, None] == segment[None, :]
    scores = jnp.where(allowed[None], scores, -1000000000.0)
    weights = jnp.exp(scores - jnp.max(scores, axis=-1, keepdims=True))
    weights = weights / jnp.sum(weights, axis=-1, keepdims=True)
    value_grad = jnp.einsum(
        "hqk,qhd->khd", weights.astype(jnp.bfloat16), cot, preferred_element_type=jnp.float32
    )
    prob_grad = jnp.einsum("qhd,khd->hqk", cot, value, preferred_element_type=jnp.float32)
    centre = jnp.sum(weights * prob_grad, axis=-1, keepdims=True)
    score_grad = (weights * (prob_grad - centre)).astype(jnp.bfloat16)
    query_grad = jnp.einsum("hqk,khd->qhd", score_grad, key, preferred_element_type=jnp.float32)
    key_grad = jnp.einsum("hqk,qhd->khd", score_grad, query, preferred_element_type=jnp.float32)

    def join(rows):
        return rows.astype(jnp.bfloat16).reshape(total, width)

    return join(value_grad), join(query_grad * scale), join(key_grad * scale)


def general_body(
    patches, norm_gain, value_weight, queries, key_vectors, head_cotangent, image_owner, patch_count
):
    devices = lax.axis_size("dp")
    rows_here = patches.shape[0]
    width = queries.shape[1]
    capacity = head_cotangent.shape[0] // devices
    segment, index = row_plan(image_owner, patch_count, rows_here, capacity, devices)
    slots = lax.all_to_all(
        head_cotangent.reshape(devices, capacity, width), "dp", split_axis=0, concat_axis=0, tiled=True
    )
    cotangent = slots.reshape(devices * capacity, width)[index]
    normed = normalize(lax.all_gather(patches, "mp", axis=1, tiled=True), norm_gain)
    values = jnp.dot(normed, value_weight, preferred_element_type=jnp.float32).astype(jnp.bfloat16)
    value_rows, query_grad, key_grad = attention_grads(
        queries, key_vectors, values, cotangent, segment
    )
    all_value_rows = lax.all_gather(value_rows, "dp", axis=0, tiled=True)
    columns = jnp.swapaxes(normed.reshape(rows_here, devices, -1), 0, 1)
    columns = lax.all_to_all(columns, "dp", split_axis=0, concat_axis=0, tiled=True)
    columns = columns.reshape(devices * rows_here, -1)
    weight_grad = lax.dot_general(
        columns, all_value_rows, (((0,), (0,)), ((), ())), preferred_element_type=jnp.float32
    )
    return weight_grad, query_grad, key_grad


def image_plan(info, row, images, capacity):
    image = jnp.zeros(row.shape, jnp.int32)
    position = jnp.zeros(row.shape, jnp.int32)
    start = jnp.int32(0)
    for index in range(images):
        end = start + info[HEADER + images + index]
        inside = (row >= start) & (row < end)
        image = jnp.where(inside, index, image)
        position = jnp.where(inside, info[HEADER + index] * capacity + row - start, position)
        start = end
    return image, position


def weights_kernel(images, info, gain_in, query_ref, key_ref, weights_ref, gain_ref):
    gain_ref[...] = gain_in[...]
    rows, width = query_ref.shape
    down = lax.broadcasted_iota(jnp.int32, (rows, rows), 0)
    across = lax.broadcasted_iota(jnp.int32, (rows, rows), 1)
    allowed = image_plan(info, down, images, 1)[0] == image_plan(info, across, images, 1)[0]
    for head in range(width // HD):
        columns = slice(head * HD, (head + 1) * HD)
        scores = lax.dot_general(
            query_ref[:, columns], key_ref[:, columns], (((1,), (1,)), ((), ())),
            preferred_element_type=jnp.float32,
        ) * (HD ** (-0.5))
        scores = jnp.where(allowed, scores, -1000000000.0)
        weights = jnp.exp(scores - jnp.max(scores, axis=-1, keepdims=True))
        weights_ref[head] = weights / jnp.sum(weights, axis=-1, keepdims=True)


def value_kernel(images, info, slots_ref, weights_ref, cot_ref, value_ref):
    slots, width = slots_ref.shape
    rows = cot_ref.shape[0]
    row = lax.broadcasted_iota(jnp.int32, (rows, slots), 0)
    _, position = image_plan(info, row, images, slots // images)
    pick = position == lax.broadcasted_iota(jnp.int32, (rows, slots), 1)
    pick = jnp.where(pick, 1.0, 0.0).astype(jnp.bfloat16)
    cot_ref[...] = jnp.dot(
        pick, slots_ref[...], preferred_element_type=jnp.float32
    ).astype(jnp.bfloat16)
    for head in range(width // HD):
        columns = slice(head * HD, (head + 1) * HD)
        value_ref[:, columns] = lax.dot_general(
            weights_ref[head].astype(jnp.bfloat16), cot_ref[:, columns], (((0,), (0,)), ((), ())),
            preferred_element_type=jnp.float32,
        ).astype(jnp.bfloat16)


def spread_of(values):
    mean = jnp.sum(values, axis=-1, keepdims=True) * (1.0 / values.shape[1])
    centred = values - mean
    return mean, jnp.sum(centred * centred, axis=-1, keepdims=True)


def stats_kernel(info, own, two, one, stats_ref, arranged):
    for index, ref in enumerate((own, one, two)):
        arranged[index ^ info[2]] = ref[...]
    rows = own.shape[0]
    lane = lax.broadcasted_iota(jnp.int32, (rows, 128), 1)
    table = jnp.zeros((rows, 128), jnp.float32)
    for index, ref in enumerate((own, one, two)):
        mean, spread = spread_of(ref[...].astype(jnp.float32))
        table = jnp.where(lane == index, mean, table)
        table = jnp.where(lane == index + 3, spread, table)
    stats_ref[...] = table


def norm_kernel(info, stats_ref, gain_ref, arranged, near, far, *rest):
    outs, halves, last_ref = rest[:8], rest[8:-1], rest[-1]
    device, layer = 2 * info[0] + info[1], info[2]
    rows, half = outs[0].shape
    last = near[...].astype(jnp.float32) + far[...].astype(jnp.float32)
    last_ref[...] = last.astype(jnp.bfloat16)
    columns = 8 * half
    last_mean, last_spread = spread_of(last)
    table = stats_ref[...]
    means = [table[:, index:index + 1] for index in range(3)] + [last_mean]
    mean = sum(means) * 0.25
    shift = sum((part - mean) * (part - mean) for part in means) * (2 * half)
    spread = table[:, 3:4] + table[:, 4:5] + table[:, 5:6] + last_spread + shift
    rstd = lax.rsqrt(spread * (1.0 / columns) + 1e-06)
    for offset, out in enumerate(outs):
        block = device ^ offset
        start = pl.multiple_of((block % 2) * half, half)
        origin = block // 2
        values = jnp.where(
            (origin ^ layer) == 3, last_ref[:, pl.ds(start, half)], arranged[origin, :, pl.ds(start, half)]
        )
        gain = gain_ref[pl.ds(block, 1), :]
        out[...] = ((values.astype(jnp.float32) - mean) * rstd * gain).astype(jnp.bfloat16)
    first = pl.multiple_of((layer % 2) * (rows // 2), rows // 2)
    for offset, ref in zip(HALVED, halves):
        ref[...] = outs[offset][pl.ds(first, rows // 2), :]


def pack_kernel(*refs):
    for index, ref in enumerate(refs[:-1]):
        refs[-1][index] = ref[...]


def project_kernel(info, weight_ref, *refs):
    normed, (value_ref, total) = refs[:8], refs[8:]
    device = 2 * info[0] + info[1]
    half = normed[0].shape[1]
    for offset, ref in enumerate(normed):
        start = pl.multiple_of((device ^ offset) * half, half)
        part = jnp.dot(ref[...], weight_ref[pl.ds(start, half), :], preferred_element_type=jnp.float32)
        if offset == 0:
            total[...] = part
        elif offset < 7:
            total[...] += part
        else:
            value_ref[...] = (total[...] + part).astype(jnp.bfloat16)


def backward_kernel(value_ref, query_ref, key_ref, cot_ref, weights_ref, query_out, key_out):
    scale = HD ** (-0.5)
    for head in range(query_ref.shape[1] // HD):
        columns = slice(head * HD, (head + 1) * HD)
        weights = weights_ref[head]
        prob_grad = lax.dot_general(
            cot_ref[:, columns], value_ref[:, columns], (((1,), (1,)), ((), ())),
            preferred_element_type=jnp.float32,
        )
        centre = jnp.sum(weights * prob_grad, axis=-1, keepdims=True)
        score_grad = (weights * (prob_grad - centre)).astype(jnp.bfloat16)
        query_out[:, columns] = (
            jnp.dot(score_grad, key_ref[:, columns], preferred_element_type=jnp.float32) * scale
        ).astype(jnp.bfloat16)
        key_out[:, columns] = (
            lax.dot_general(
                score_grad, query_ref[:, columns], (((0,), (0,)), ((), ())),
                preferred_element_type=jnp.float32,
            ) * scale
        ).astype(jnp.bfloat16)


def joined(info, names, refs):
    refs = list(refs)
    chip_values, mate_values = refs[-5:-1], refs[-1]
    left, right = [], []

    def rows_of(offset, swapped=None):
        values = mate_values.at[offset // 2] if offset % 2 else chip_values[offset // 2]
        if swapped is None:
            return values[...]
        rows = values.shape[0] // 2
        side = (info[2] + swapped) % 2
        return values[pl.ds(pl.multiple_of(side * rows, rows), rows), :]

    for name in names:
        left.append(refs.pop(0)[...])
        if name == SWAPPED:
            right.extend(rows_of(offset, 1) for offset in HALVED)
        else:
            right.append(rows_of(name, 0 if name in HALVED else None))
    return jnp.concatenate(left, axis=0), jnp.concatenate(right, axis=0)


def gradient_first_kernel(names, info, *refs):
    left, right = joined(info, names, refs[:-1])
    refs[-1][...] = lax.dot_general(
        left, right, (((0,), (0,)), ((), ())), preferred_element_type=jnp.float32
    )


def gradient_last_kernel(names, info, before, *refs):
    left, right = joined(info, names, refs[:-3])
    out_ref, ready, done = refs[-3:]
    blocks, rows, _ = ready.shape
    copies = []
    for block in range(blocks):
        part = slice(block * rows, (block + 1) * rows)
        ready[block] = before[part, :] + lax.dot_general(
            left[:, part], right, (((0,), (0,)), ((), ())), preferred_element_type=jnp.float32
        )
        copies.append(
            pltpu.make_async_copy(ready.at[block], out_ref.at[pl.ds(block * rows, rows)], done.at[block])
        )
        copies[-1].start()
    for copy in copies:
        copy.wait()


def shape(dims, dtype=jnp.bfloat16):
    return jax.ShapeDtypeStruct(dims, dtype)


VMEM_LIMIT = 24 * 1024 * 1024
BIG = 56 * 1024 * 1024
SMEM = pl.BlockSpec(memory_space=pltpu.SMEM)
WHOLE = pl.BlockSpec(memory_space=pltpu.VMEM)
ANY = pl.BlockSpec(memory_space=pl.ANY)


def call(kernel, name, out_shape, in_specs, out_specs, scratch=(), limit=VMEM_LIMIT, after=()):
    used = len(in_specs)

    def body(*refs):
        return kernel(*refs[:used], *refs[used + len(after):])

    made = pl.pallas_call(
        body,
        name=name,
        out_shape=out_shape,
        in_specs=list(in_specs) + [ANY] * len(after),
        out_specs=out_specs,
        scratch_shapes=list(scratch),
        cost_estimate=pl.CostEstimate(flops=1, bytes_accessed=1, transcendentals=0),
        compiler_params=pltpu.CompilerParams(vmem_limit_bytes=limit),
    )
    return lambda *args: made(*args, *after)


def across(rows, distance):
    return lax.ppermute(rows, "dp", [(i, i ^ distance) for i in range(8)])


def between_chips(blocks):
    return lax.all_to_all(
        blocks, "dp", split_axis=0, concat_axis=0, tiled=True,
        axis_index_groups=[[0, 2, 4, 6], [1, 3, 5, 7]],
    )


def fast_body(
    patches, norm_gain, value_weight, queries, key_vectors, head_cotangent, image_owner, patch_count
):
    rows, columns = patches.shape
    half = columns // 2
    width = queries.shape[1]
    heads = width // HD
    images = image_owner.shape[1]
    slots = head_cotangent.shape[0]
    device = lax.axis_index("dp").astype(jnp.int32)
    place = [device // 2, device % 2, lax.axis_index("mp").astype(jnp.int32)]
    info = jnp.concatenate([
        jnp.stack(place + [jnp.int32(0)] * (HEADER - 3)),
        lax.dynamic_index_in_dim(image_owner, device, 0, keepdims=False),
        lax.dynamic_index_in_dim(patch_count, device, 0, keepdims=False),
    ])
    flat = (rows, width)

    received = lax.all_to_all(
        head_cotangent.reshape(8, slots // 8, width), "dp", split_axis=0, concat_axis=0, tiled=True
    ).reshape(slots, width)
    two = lax.ppermute(patches, "mp", [(0, 2), (2, 0), (1, 3), (3, 1)])
    one = lax.ppermute(patches, "mp", [(0, 1), (1, 0), (2, 3), (3, 2)])

    weights, gain = call(
        functools.partial(weights_kernel, images), "attention_weights",
        (shape((heads, rows, rows), jnp.float32), shape((8, half), jnp.float32)), [SMEM] + [WHOLE] * 3, (WHOLE, WHOLE),
    )(info, norm_gain.reshape(8, half), queries, key_vectors)
    cotangent, value_rows = call(
        functools.partial(value_kernel, images), "value_rows",
        (shape(flat), shape(flat)), [SMEM, WHOLE, WHOLE], (WHOLE, WHOLE),
    )(info, received, weights)
    middle, passed, first_one, _ = lax.optimization_barrier((patches, two, one, value_rows))
    near = lax.ppermute(middle, "mp", [(1, 2), (2, 1)])
    far = lax.ppermute(passed, "mp", [(2, 3), (1, 0)])
    chip_values = [value_rows] + [across(value_rows, distance) for distance in (2, 4, 6)]

    block = shape((rows, half))
    stats, arranged = call(
        stats_kernel, "partial_stats", (shape((rows, 128), jnp.float32), shape((4, rows, columns))),
        [SMEM] + [WHOLE] * 3, (WHOLE, WHOLE), after=(value_weight,),
    )(info, middle, passed, first_one)
    *normed, = call(
        norm_kernel, "norm_rows", (block,) * 8 + (shape((rows // 2, half)),) * len(HALVED),
        [SMEM] + [WHOLE] * 5, (WHOLE,) * (8 + len(HALVED)), (pltpu.VMEM((rows, columns), jnp.bfloat16),),
    )(info, stats, gain, arranged, near, far)
    normed, halves = normed[:8], normed[8:]
    packed = call(pack_kernel, "pack_values", shape((4,) + flat), [WHOLE] * 4, WHOLE, after=(normed[1],))(*chip_values)

    mate_values = across(packed, 1)
    mate_rows = across(normed[1], 1)
    values = call(
        project_kernel, "project_values", shape(flat), [SMEM] + [WHOLE] * 9, WHOLE, (pltpu.VMEM(flat, jnp.float32),),
        after=(mate_values, mate_rows),
    )(info, value_weight, *normed)
    query_grad, key_grad = call(
        backward_kernel, "attention_backward", (shape(flat), shape(flat)), [WHOLE] * 5, (WHOLE,) * 2,
    )(values, queries, key_vectors, cotangent, weights)

    moved = {0: normed[0], 1: mate_rows}
    sources = {offset: normed[offset] for offset in range(2, 8)} | dict(zip(HALVED, halves))
    for offset in range(2, 8):
        if offset not in LATE:
            moved[offset] = across(sources[offset], offset)
    swapped = call(pack_kernel, "pack_halves", shape((2, rows // 2, half)), [WHOLE] * 2, WHOLE, after=(values,))(
        *[moved[offset] for offset in HALVED]
    )
    sources[SWAPPED] = swapped.reshape(rows, half)
    held = lax.optimization_barrier([sources[name] for name in LATE] + [values])
    for name, part in zip(LATE, held):
        if name == SWAPPED:
            moved[name] = lax.ppermute(part, "mp", [(0, 1), (1, 0), (2, 3), (3, 2)])
        else:
            moved[name] = across(part, name)

    def arrived(names):
        return [moved[name] for name in names] + chip_values + [mate_values]

    grad = shape((half, width), jnp.float32)
    parts = arrived(FIRST)
    partial = call(
        functools.partial(gradient_first_kernel, FIRST), "gradient_first", grad, [SMEM] + [WHOLE] * len(parts), WHOLE
    )(info, *parts)
    parts = arrived(LAST)
    blocks = half // 256
    weight_grad = call(
        functools.partial(gradient_last_kernel, LAST), "gradient_last", grad, [SMEM] + [WHOLE] * (len(parts) + 1), ANY,
        (pltpu.VMEM((blocks, 256, width), jnp.float32), pltpu.SemaphoreType.DMA((blocks,))),
        after=(query_grad,),
    )(info, partial, *parts)
    return weight_grad, query_grad, key_grad


def solution(mesh):
    fast = mesh.shape["dp"] == 8 and mesh.shape["mp"] == 4
    return jax.shard_map(
        fast_body if fast else general_body,
        mesh=mesh,
        in_specs=(
            P("dp", "mp"),
            P(),
            P(None, "mp"),
            P("dp", "mp"),
            P("dp", "mp"),
            P("dp", "mp"),
            P(),
            P(),
        ),
        out_specs=(P("dp", "mp"), P("dp", "mp"), P("dp", "mp")),
        check_vma=False,
    )
```

```python
import functools

import jax
import jax.numpy as jnp
from jax import lax
from jax.experimental import pallas as pl
from jax.experimental.pallas import tpu as pltpu
from jax.sharding import PartitionSpec as P

HD = 128
HEADER = 8
FIRST = (0,6,7,2,4,1)
LAST = (20,3,5)
LATE = (20,3,5)
HALVED = (6, 7)
SWAPPED = 20


def normalize(rows, norm_gain):
    values = rows.astype(jnp.float32)
    average = jnp.mean(values, axis=-1, keepdims=True)
    centred = values - average
    variance = jnp.mean(centred * centred, axis=-1, keepdims=True)
    return (centred * lax.rsqrt(variance + 1e-06) * norm_gain).astype(jnp.bfloat16)


def row_plan(image_owner, patch_count, rows_here, capacity, devices):
    device = lax.axis_index("dp")
    own_list = lax.dynamic_index_in_dim(image_owner, device, 0, keepdims=False)
    own_count = lax.dynamic_index_in_dim(patch_count, device, 0, keepdims=False)
    ends = jnp.cumsum(own_count)
    starts = ends - own_count
    row_index = jnp.arange(rows_here, dtype=jnp.int32)
    image_of = jnp.sum((ends[None, :] <= row_index[:, None]).astype(jnp.int32), axis=1)
    picked = image_of[:, None] == jnp.arange(devices, dtype=jnp.int32)[None, :]
    row_owner = jnp.sum(jnp.where(picked, own_list[None, :], 0), axis=1)
    row_start = jnp.sum(jnp.where(picked, starts[None, :], 0), axis=1)
    return image_of, row_owner * capacity + row_index - row_start


def attention_grads(query_rows, key_rows, value_rows, cotangent, segment):
    total, width = query_rows.shape
    heads = width // HD
    scale = HD ** (-0.5)

    def split(rows):
        return rows.reshape(total, heads, HD)

    query, key, value, cot = split(query_rows), split(key_rows), split(value_rows), split(cotangent)
    scores = jnp.einsum("qhd,khd->hqk", query, key, preferred_element_type=jnp.float32) * scale
    allowed = segment[:, None] == segment[None, :]
    scores = jnp.where(allowed[None], scores, -1000000000.0)
    weights = jnp.exp(scores - jnp.max(scores, axis=-1, keepdims=True))
    weights = weights / jnp.sum(weights, axis=-1, keepdims=True)
    value_grad = jnp.einsum(
        "hqk,qhd->khd", weights.astype(jnp.bfloat16), cot, preferred_element_type=jnp.float32
    )
    prob_grad = jnp.einsum("qhd,khd->hqk", cot, value, preferred_element_type=jnp.float32)
    centre = jnp.sum(weights * prob_grad, axis=-1, keepdims=True)
    score_grad = (weights * (prob_grad - centre)).astype(jnp.bfloat16)
    query_grad = jnp.einsum("hqk,khd->qhd", score_grad, key, preferred_element_type=jnp.float32)
    key_grad = jnp.einsum("hqk,qhd->khd", score_grad, query, preferred_element_type=jnp.float32)

    def join(rows):
        return rows.astype(jnp.bfloat16).reshape(total, width)

    return join(value_grad), join(query_grad * scale), join(key_grad * scale)


def general_body(
    patches, norm_gain, value_weight, queries, key_vectors, head_cotangent, image_owner, patch_count
):
    devices = lax.axis_size("dp")
    rows_here = patches.shape[0]
    width = queries.shape[1]
    capacity = head_cotangent.shape[0] // devices
    segment, index = row_plan(image_owner, patch_count, rows_here, capacity, devices)
    slots = lax.all_to_all(
        head_cotangent.reshape(devices, capacity, width), "dp", split_axis=0, concat_axis=0, tiled=True
    )
    cotangent = slots.reshape(devices * capacity, width)[index]
    normed = normalize(lax.all_gather(patches, "mp", axis=1, tiled=True), norm_gain)
    values = jnp.dot(normed, value_weight, preferred_element_type=jnp.float32).astype(jnp.bfloat16)
    value_rows, query_grad, key_grad = attention_grads(
        queries, key_vectors, values, cotangent, segment
    )
    all_value_rows = lax.all_gather(value_rows, "dp", axis=0, tiled=True)
    columns = jnp.swapaxes(normed.reshape(rows_here, devices, -1), 0, 1)
    columns = lax.all_to_all(columns, "dp", split_axis=0, concat_axis=0, tiled=True)
    columns = columns.reshape(devices * rows_here, -1)
    weight_grad = lax.dot_general(
        columns, all_value_rows, (((0,), (0,)), ((), ())), preferred_element_type=jnp.float32
    )
    return weight_grad, query_grad, key_grad


def image_plan(info, row, images, capacity):
    image = jnp.zeros(row.shape, jnp.int32)
    position = jnp.zeros(row.shape, jnp.int32)
    start = jnp.int32(0)
    for index in range(images):
        end = start + info[HEADER + images + index]
        inside = (row >= start) & (row < end)
        image = jnp.where(inside, index, image)
        position = jnp.where(inside, info[HEADER + index] * capacity + row - start, position)
        start = end
    return image, position


def weights_kernel(images, info, gain_in, query_ref, key_ref, weights_ref, gain_ref):
    gain_ref[...] = gain_in[...]
    rows, width = query_ref.shape
    down = lax.broadcasted_iota(jnp.int32, (rows, rows), 0)
    across = lax.broadcasted_iota(jnp.int32, (rows, rows), 1)
    allowed = image_plan(info, down, images, 1)[0] == image_plan(info, across, images, 1)[0]
    for head in range(width // HD):
        columns = slice(head * HD, (head + 1) * HD)
        scores = lax.dot_general(
            query_ref[:, columns], key_ref[:, columns], (((1,), (1,)), ((), ())),
            preferred_element_type=jnp.float32,
        ) * (HD ** (-0.5))
        scores = jnp.where(allowed, scores, -1000000000.0)
        weights = jnp.exp(scores - jnp.max(scores, axis=-1, keepdims=True))
        weights_ref[head] = weights / jnp.sum(weights, axis=-1, keepdims=True)


def value_kernel(images, info, slots_ref, weights_ref, cot_ref, value_ref):
    slots, width = slots_ref.shape
    rows = cot_ref.shape[0]
    row = lax.broadcasted_iota(jnp.int32, (rows, slots), 0)
    _, position = image_plan(info, row, images, slots // images)
    pick = position == lax.broadcasted_iota(jnp.int32, (rows, slots), 1)
    pick = jnp.where(pick, 1.0, 0.0).astype(jnp.bfloat16)
    cot_ref[...] = jnp.dot(
        pick, slots_ref[...], preferred_element_type=jnp.float32
    ).astype(jnp.bfloat16)
    for head in range(width // HD):
        columns = slice(head * HD, (head + 1) * HD)
        value_ref[:, columns] = lax.dot_general(
            weights_ref[head].astype(jnp.bfloat16), cot_ref[:, columns], (((0,), (0,)), ((), ())),
            preferred_element_type=jnp.float32,
        ).astype(jnp.bfloat16)


def spread_of(values):
    mean = jnp.sum(values, axis=-1, keepdims=True) * (1.0 / values.shape[1])
    centred = values - mean
    return mean, jnp.sum(centred * centred, axis=-1, keepdims=True)


def stats_kernel(info, own, two, one, stats_ref, arranged):
    for index, ref in enumerate((own, one, two)):
        arranged[index ^ info[2]] = ref[...]
    rows = own.shape[0]
    lane = lax.broadcasted_iota(jnp.int32, (rows, 128), 1)
    table = jnp.zeros((rows, 128), jnp.float32)
    for index, ref in enumerate((own, one, two)):
        mean, spread = spread_of(ref[...].astype(jnp.float32))
        table = jnp.where(lane == index, mean, table)
        table = jnp.where(lane == index + 3, spread, table)
    stats_ref[...] = table


def norm_kernel(info, stats_ref, gain_ref, arranged, near, far, *rest):
    outs, halves, last_ref = rest[:8], rest[8:-1], rest[-1]
    device, layer = 2 * info[0] + info[1], info[2]
    rows, half = outs[0].shape
    last = near[...].astype(jnp.float32) + far[...].astype(jnp.float32)
    last_ref[...] = last.astype(jnp.bfloat16)
    columns = 8 * half
    last_mean, last_spread = spread_of(last)
    table = stats_ref[...]
    means = [table[:, index:index + 1] for index in range(3)] + [last_mean]
    mean = sum(means) * 0.25
    shift = sum((part - mean) * (part - mean) for part in means) * (2 * half)
    spread = table[:, 3:4] + table[:, 4:5] + table[:, 5:6] + last_spread + shift
    rstd = lax.rsqrt(spread * (1.0 / columns) + 1e-06)
    for offset, out in enumerate(outs):
        block = device ^ offset
        start = pl.multiple_of((block % 2) * half, half)
        origin = block // 2
        values = jnp.where(
            (origin ^ layer) == 3, last_ref[:, pl.ds(start, half)], arranged[origin, :, pl.ds(start, half)]
        )
        gain = gain_ref[pl.ds(block, 1), :]
        out[...] = ((values.astype(jnp.float32) - mean) * rstd * gain).astype(jnp.bfloat16)
    first = pl.multiple_of((layer % 2) * (rows // 2), rows // 2)
    for offset, ref in zip(HALVED, halves):
        ref[...] = outs[offset][pl.ds(first, rows // 2), :]


def pack_kernel(*refs):
    for index, ref in enumerate(refs[:-1]):
        refs[-1][index] = ref[...]


def project_kernel(info, weight_ref, *refs):
    normed, (value_ref, total) = refs[:8], refs[8:]
    device = 2 * info[0] + info[1]
    half = normed[0].shape[1]
    for offset, ref in enumerate(normed):
        start = pl.multiple_of((device ^ offset) * half, half)
        part = jnp.dot(ref[...], weight_ref[pl.ds(start, half), :], preferred_element_type=jnp.float32)
        if offset == 0:
            total[...] = part
        elif offset < 7:
            total[...] += part
        else:
            value_ref[...] = (total[...] + part).astype(jnp.bfloat16)


def backward_kernel(value_ref, query_ref, key_ref, cot_ref, weights_ref, query_out, key_out):
    scale = HD ** (-0.5)
    for head in range(query_ref.shape[1] // HD):
        columns = slice(head * HD, (head + 1) * HD)
        weights = weights_ref[head]
        prob_grad = lax.dot_general(
            cot_ref[:, columns], value_ref[:, columns], (((1,), (1,)), ((), ())),
            preferred_element_type=jnp.float32,
        )
        centre = jnp.sum(weights * prob_grad, axis=-1, keepdims=True)
        score_grad = (weights * (prob_grad - centre)).astype(jnp.bfloat16)
        query_out[:, columns] = (
            jnp.dot(score_grad, key_ref[:, columns], preferred_element_type=jnp.float32) * scale
        ).astype(jnp.bfloat16)
        key_out[:, columns] = (
            lax.dot_general(
                score_grad, query_ref[:, columns], (((0,), (0,)), ((), ())),
                preferred_element_type=jnp.float32,
            ) * scale
        ).astype(jnp.bfloat16)


def value_parts(info, names, chip_values, mate_values):
    parts = []

    def rows_of(offset, swapped=None):
        values = mate_values.at[offset // 2] if offset % 2 else chip_values[offset // 2]
        if swapped is None:
            return values[...]
        rows = values.shape[0] // 2
        side = (info[2] + swapped) % 2
        return values[pl.ds(pl.multiple_of(side * rows, rows), rows), :]

    for name in names:
        if name == SWAPPED:
            parts.extend(rows_of(offset, 1) for offset in HALVED)
        else:
            parts.append(rows_of(name, 0 if name in HALVED else None))
    return parts


def gradient_first_kernel(info, *refs):
    normed, chip_values, mate_values = refs[:-7], refs[-7:-3], refs[-3]
    sum_ref, right_ref = refs[-2:]
    row = 0
    for part in value_parts(info, LAST, chip_values, mate_values):
        right_ref[row:row + part.shape[0], :] = part
        row += part.shape[0]
    left = jnp.concatenate([ref[...] for ref in normed], axis=0)
    right = jnp.concatenate(value_parts(info, FIRST, chip_values, mate_values), axis=0)
    sum_ref[...] = lax.dot_general(
        left, right, (((0,), (0,)), ((), ())), preferred_element_type=jnp.float32
    )


def gradient_last_kernel(before, right, *refs):
    normed, (out_ref, ready, done) = refs[:-3], refs[-3:]
    left = jnp.concatenate([ref[...] for ref in normed], axis=0)
    blocks, rows, _ = ready.shape
    copies = []
    for block in range(blocks):
        part = slice(block * rows, (block + 1) * rows)
        ready[block] = before[part, :] + lax.dot_general(
            left[:, part], right[...], (((0,), (0,)), ((), ())), preferred_element_type=jnp.float32
        )
        copies.append(
            pltpu.make_async_copy(ready.at[block], out_ref.at[pl.ds(block * rows, rows)], done.at[block])
        )
        copies[-1].start()
    for copy in copies:
        copy.wait()


def shape(dims, dtype=jnp.bfloat16):
    return jax.ShapeDtypeStruct(dims, dtype)


VMEM_LIMIT = 24 * 1024 * 1024
BIG = 56 * 1024 * 1024
SMEM = pl.BlockSpec(memory_space=pltpu.SMEM)
WHOLE = pl.BlockSpec(memory_space=pltpu.VMEM)
ANY = pl.BlockSpec(memory_space=pl.ANY)


def call(kernel, name, out_shape, in_specs, out_specs, scratch=(), limit=VMEM_LIMIT, after=()):
    used = len(in_specs)

    def body(*refs):
        return kernel(*refs[:used], *refs[used + len(after):])

    made = pl.pallas_call(
        body,
        name=name,
        out_shape=out_shape,
        in_specs=list(in_specs) + [ANY] * len(after),
        out_specs=out_specs,
        scratch_shapes=list(scratch),
        cost_estimate=pl.CostEstimate(flops=1, bytes_accessed=1, transcendentals=0),
        compiler_params=pltpu.CompilerParams(vmem_limit_bytes=limit),
    )
    return lambda *args: made(*args, *after)


def across(rows, distance):
    return lax.ppermute(rows, "dp", [(i, i ^ distance) for i in range(8)])


def between_chips(blocks):
    return lax.all_to_all(
        blocks, "dp", split_axis=0, concat_axis=0, tiled=True,
        axis_index_groups=[[0, 2, 4, 6], [1, 3, 5, 7]],
    )


def fast_body(
    patches, norm_gain, value_weight, queries, key_vectors, head_cotangent, image_owner, patch_count
):
    rows, columns = patches.shape
    half = columns // 2
    width = queries.shape[1]
    heads = width // HD
    images = image_owner.shape[1]
    slots = head_cotangent.shape[0]
    device = lax.axis_index("dp").astype(jnp.int32)
    place = [device // 2, device % 2, lax.axis_index("mp").astype(jnp.int32)]
    info = jnp.concatenate([
        jnp.stack(place + [jnp.int32(0)] * (HEADER - 3)),
        lax.dynamic_index_in_dim(image_owner, device, 0, keepdims=False),
        lax.dynamic_index_in_dim(patch_count, device, 0, keepdims=False),
    ])
    flat = (rows, width)

    received = lax.all_to_all(
        head_cotangent.reshape(8, slots // 8, width), "dp", split_axis=0, concat_axis=0, tiled=True
    ).reshape(slots, width)
    two = lax.ppermute(patches, "mp", [(0, 2), (2, 0), (1, 3), (3, 1)])
    one = lax.ppermute(patches, "mp", [(0, 1), (1, 0), (2, 3), (3, 2)])

    weights, gain = call(
        functools.partial(weights_kernel, images), "attention_weights",
        (shape((heads, rows, rows), jnp.float32), shape((8, half), jnp.float32)), [SMEM] + [WHOLE] * 3, (WHOLE, WHOLE),
    )(info, norm_gain.reshape(8, half), queries, key_vectors)
    cotangent, value_rows = call(
        functools.partial(value_kernel, images), "value_rows",
        (shape(flat), shape(flat)), [SMEM, WHOLE, WHOLE], (WHOLE, WHOLE),
    )(info, received, weights)
    middle, passed, first_one, _ = lax.optimization_barrier((patches, two, one, value_rows))
    near = lax.ppermute(middle, "mp", [(1, 2), (2, 1)])
    far = lax.ppermute(passed, "mp", [(2, 3), (1, 0)])
    chip_values = [value_rows] + [across(value_rows, distance) for distance in (2, 4, 6)]

    block = shape((rows, half))
    stats, arranged = call(
        stats_kernel, "partial_stats", (shape((rows, 128), jnp.float32), shape((4, rows, columns))),
        [SMEM] + [WHOLE] * 3, (WHOLE, WHOLE), after=(value_weight,),
    )(info, middle, passed, first_one)
    *normed, = call(
        norm_kernel, "norm_rows", (block,) * 8 + (shape((rows // 2, half)),) * len(HALVED),
        [SMEM] + [WHOLE] * 5, (WHOLE,) * (8 + len(HALVED)), (pltpu.VMEM((rows, columns), jnp.bfloat16),),
    )(info, stats, gain, arranged, near, far)
    normed, halves = normed[:8], normed[8:]
    packed = call(pack_kernel, "pack_values", shape((4,) + flat), [WHOLE] * 4, WHOLE, after=(normed[1],))(*chip_values)

    mate_values = across(packed, 1)
    mate_rows = across(normed[1], 1)
    values = call(
        project_kernel, "project_values", shape(flat), [SMEM] + [WHOLE] * 9, WHOLE, (pltpu.VMEM(flat, jnp.float32),),
        after=(mate_values, mate_rows),
    )(info, value_weight, *normed)
    query_grad, key_grad = call(
        backward_kernel, "attention_backward", (shape(flat), shape(flat)), [WHOLE] * 5, (WHOLE,) * 2,
    )(values, queries, key_vectors, cotangent, weights)

    moved = {0: normed[0], 1: mate_rows}
    sources = {offset: normed[offset] for offset in range(2, 8)} | dict(zip(HALVED, halves))
    for offset in range(2, 8):
        if offset not in LATE:
            moved[offset] = across(sources[offset], offset)
    swapped = call(pack_kernel, "pack_halves", shape((2, rows // 2, half)), [WHOLE] * 2, WHOLE, after=(values,))(
        *[moved[offset] for offset in HALVED]
    )
    sources[SWAPPED] = swapped.reshape(rows, half)
    held = lax.optimization_barrier([sources[name] for name in LATE] + [values])
    for name, part in zip(LATE, held):
        if name == SWAPPED:
            moved[name] = lax.ppermute(part, "mp", [(0, 1), (1, 0), (2, 3), (3, 2)])
        else:
            moved[name] = across(part, name)

    first, last = [moved[name] for name in FIRST], [moved[name] for name in LAST]
    grad = shape((half, width), jnp.float32)
    partial, last_values = call(
        gradient_first_kernel, "gradient_first", (grad, shape((rows * len(LAST), width))),
        [SMEM] + [WHOLE] * (len(first) + 5), (WHOLE, WHOLE),
    )(info, *first, *chip_values, mate_values)
    blocks = half // 256
    weight_grad = call(
        gradient_last_kernel, "gradient_last", grad, [WHOLE] * (len(last) + 2), ANY,
        (pltpu.VMEM((blocks, 256, width), jnp.float32), pltpu.SemaphoreType.DMA((blocks,))),
        after=(query_grad,),
    )(partial, last_values, *last)
    return weight_grad, query_grad, key_grad


def solution(mesh):
    fast = mesh.shape["dp"] == 8 and mesh.shape["mp"] == 4
    return jax.shard_map(
        fast_body if fast else general_body,
        mesh=mesh,
        in_specs=(
            P("dp", "mp"),
            P(),
            P(None, "mp"),
            P("dp", "mp"),
            P("dp", "mp"),
            P("dp", "mp"),
            P(),
            P(),
        ),
        out_specs=(P("dp", "mp"), P("dp", "mp"), P("dp", "mp")),
        check_vma=False,
    )
```

```python
import functools

import jax
import jax.numpy as jnp
from jax import lax
from jax.experimental import pallas as pl
from jax.experimental.pallas import tpu as pltpu
from jax.sharding import PartitionSpec as P

HD = 128
HEADER = 8
FIRST = (0,6,7,2,4,1)
LAST = (20,3,5)
LATE = (20,3,5)
HALVED = (6, 7)
SWAPPED = 20


def normalize(rows, norm_gain):
    values = rows.astype(jnp.float32)
    average = jnp.mean(values, axis=-1, keepdims=True)
    centred = values - average
    variance = jnp.mean(centred * centred, axis=-1, keepdims=True)
    return (centred * lax.rsqrt(variance + 1e-06) * norm_gain).astype(jnp.bfloat16)


def row_plan(image_owner, patch_count, rows_here, capacity, devices):
    device = lax.axis_index("dp")
    own_list = lax.dynamic_index_in_dim(image_owner, device, 0, keepdims=False)
    own_count = lax.dynamic_index_in_dim(patch_count, device, 0, keepdims=False)
    ends = jnp.cumsum(own_count)
    starts = ends - own_count
    row_index = jnp.arange(rows_here, dtype=jnp.int32)
    image_of = jnp.sum((ends[None, :] <= row_index[:, None]).astype(jnp.int32), axis=1)
    picked = image_of[:, None] == jnp.arange(devices, dtype=jnp.int32)[None, :]
    row_owner = jnp.sum(jnp.where(picked, own_list[None, :], 0), axis=1)
    row_start = jnp.sum(jnp.where(picked, starts[None, :], 0), axis=1)
    return image_of, row_owner * capacity + row_index - row_start


def attention_grads(query_rows, key_rows, value_rows, cotangent, segment):
    total, width = query_rows.shape
    heads = width // HD
    scale = HD ** (-0.5)

    def split(rows):
        return rows.reshape(total, heads, HD)

    query, key, value, cot = split(query_rows), split(key_rows), split(value_rows), split(cotangent)
    scores = jnp.einsum("qhd,khd->hqk", query, key, preferred_element_type=jnp.float32) * scale
    allowed = segment[:, None] == segment[None, :]
    scores = jnp.where(allowed[None], scores, -1000000000.0)
    weights = jnp.exp(scores - jnp.max(scores, axis=-1, keepdims=True))
    weights = weights / jnp.sum(weights, axis=-1, keepdims=True)
    value_grad = jnp.einsum(
        "hqk,qhd->khd", weights.astype(jnp.bfloat16), cot, preferred_element_type=jnp.float32
    )
    prob_grad = jnp.einsum("qhd,khd->hqk", cot, value, preferred_element_type=jnp.float32)
    centre = jnp.sum(weights * prob_grad, axis=-1, keepdims=True)
    score_grad = (weights * (prob_grad - centre)).astype(jnp.bfloat16)
    query_grad = jnp.einsum("hqk,khd->qhd", score_grad, key, preferred_element_type=jnp.float32)
    key_grad = jnp.einsum("hqk,qhd->khd", score_grad, query, preferred_element_type=jnp.float32)

    def join(rows):
        return rows.astype(jnp.bfloat16).reshape(total, width)

    return join(value_grad), join(query_grad * scale), join(key_grad * scale)


def general_body(
    patches, norm_gain, value_weight, queries, key_vectors, head_cotangent, image_owner, patch_count
):
    devices = lax.axis_size("dp")
    rows_here = patches.shape[0]
    width = queries.shape[1]
    capacity = head_cotangent.shape[0] // devices
    segment, index = row_plan(image_owner, patch_count, rows_here, capacity, devices)
    slots = lax.all_to_all(
        head_cotangent.reshape(devices, capacity, width), "dp", split_axis=0, concat_axis=0, tiled=True
    )
    cotangent = slots.reshape(devices * capacity, width)[index]
    normed = normalize(lax.all_gather(patches, "mp", axis=1, tiled=True), norm_gain)
    values = jnp.dot(normed, value_weight, preferred_element_type=jnp.float32).astype(jnp.bfloat16)
    value_rows, query_grad, key_grad = attention_grads(
        queries, key_vectors, values, cotangent, segment
    )
    all_value_rows = lax.all_gather(value_rows, "dp", axis=0, tiled=True)
    columns = jnp.swapaxes(normed.reshape(rows_here, devices, -1), 0, 1)
    columns = lax.all_to_all(columns, "dp", split_axis=0, concat_axis=0, tiled=True)
    columns = columns.reshape(devices * rows_here, -1)
    weight_grad = lax.dot_general(
        columns, all_value_rows, (((0,), (0,)), ((), ())), preferred_element_type=jnp.float32
    )
    return weight_grad, query_grad, key_grad


def image_plan(info, row, images, capacity):
    image = jnp.zeros(row.shape, jnp.int32)
    position = jnp.zeros(row.shape, jnp.int32)
    start = jnp.int32(0)
    for index in range(images):
        end = start + info[HEADER + images + index]
        inside = (row >= start) & (row < end)
        image = jnp.where(inside, index, image)
        position = jnp.where(inside, info[HEADER + index] * capacity + row - start, position)
        start = end
    return image, position


def weights_kernel(images, info, gain_in, query_ref, key_ref, weights_ref, gain_ref):
    gain_ref[...] = gain_in[...]
    rows, width = query_ref.shape
    down = lax.broadcasted_iota(jnp.int32, (rows, rows), 0)
    across = lax.broadcasted_iota(jnp.int32, (rows, rows), 1)
    allowed = image_plan(info, down, images, 1)[0] == image_plan(info, across, images, 1)[0]
    for head in range(width // HD):
        columns = slice(head * HD, (head + 1) * HD)
        scores = lax.dot_general(
            query_ref[:, columns], key_ref[:, columns], (((1,), (1,)), ((), ())),
            preferred_element_type=jnp.float32,
        ) * (HD ** (-0.5))
        scores = jnp.where(allowed, scores, -1000000000.0)
        weights = jnp.exp(scores - jnp.max(scores, axis=-1, keepdims=True))
        weights_ref[head] = weights / jnp.sum(weights, axis=-1, keepdims=True)


def value_kernel(images, info, slots_ref, weights_ref, cot_ref, value_ref):
    slots, width = slots_ref.shape
    rows = cot_ref.shape[0]
    row = lax.broadcasted_iota(jnp.int32, (rows, slots), 0)
    _, position = image_plan(info, row, images, slots // images)
    pick = position == lax.broadcasted_iota(jnp.int32, (rows, slots), 1)
    pick = jnp.where(pick, 1.0, 0.0).astype(jnp.bfloat16)
    cot_ref[...] = jnp.dot(
        pick, slots_ref[...], preferred_element_type=jnp.float32
    ).astype(jnp.bfloat16)
    for head in range(width // HD):
        columns = slice(head * HD, (head + 1) * HD)
        value_ref[:, columns] = lax.dot_general(
            weights_ref[head].astype(jnp.bfloat16), cot_ref[:, columns], (((0,), (0,)), ((), ())),
            preferred_element_type=jnp.float32,
        ).astype(jnp.bfloat16)


def spread_of(values):
    mean = jnp.sum(values, axis=-1, keepdims=True) * (1.0 / values.shape[1])
    centred = values - mean
    return mean, jnp.sum(centred * centred, axis=-1, keepdims=True)


def stats_kernel(info, own, two, one, stats_ref, arranged):
    for index, ref in enumerate((own, one, two)):
        arranged[index ^ info[2]] = ref[...]
    rows = own.shape[0]
    lane = lax.broadcasted_iota(jnp.int32, (rows, 128), 1)
    table = jnp.zeros((rows, 128), jnp.float32)
    for index, ref in enumerate((own, one, two)):
        mean, spread = spread_of(ref[...].astype(jnp.float32))
        table = jnp.where(lane == index, mean, table)
        table = jnp.where(lane == index + 3, spread, table)
    stats_ref[...] = table


def norm_kernel(info, stats_ref, gain_ref, arranged, near, far, *rest):
    outs, halves, last_ref = rest[:8], rest[8:-1], rest[-1]
    device, layer = 2 * info[0] + info[1], info[2]
    rows, half = outs[0].shape
    last = near[...].astype(jnp.float32) + far[...].astype(jnp.float32)
    last_ref[...] = last.astype(jnp.bfloat16)
    columns = 8 * half
    last_mean, last_spread = spread_of(last)
    table = stats_ref[...]
    means = [table[:, index:index + 1] for index in range(3)] + [last_mean]
    mean = sum(means) * 0.25
    shift = sum((part - mean) * (part - mean) for part in means) * (2 * half)
    spread = table[:, 3:4] + table[:, 4:5] + table[:, 5:6] + last_spread + shift
    rstd = lax.rsqrt(spread * (1.0 / columns) + 1e-06)
    for offset, out in enumerate(outs):
        block = device ^ offset
        start = pl.multiple_of((block % 2) * half, half)
        origin = block // 2
        values = jnp.where(
            (origin ^ layer) == 3, last_ref[:, pl.ds(start, half)], arranged[origin, :, pl.ds(start, half)]
        )
        gain = gain_ref[pl.ds(block, 1), :]
        out[...] = ((values.astype(jnp.float32) - mean) * rstd * gain).astype(jnp.bfloat16)
    first = pl.multiple_of((layer % 2) * (rows // 2), rows // 2)
    for offset, ref in zip(HALVED, halves):
        ref[...] = outs[offset][pl.ds(first, rows // 2), :]


def pack_kernel(*refs):
    for index, ref in enumerate(refs[:-1]):
        refs[-1][index] = ref[...]


def project_kernel(info, weight_ref, *refs):
    normed, (value_ref, total) = refs[:8], refs[8:]
    device = 2 * info[0] + info[1]
    half = normed[0].shape[1]
    for offset, ref in enumerate(normed):
        start = pl.multiple_of((device ^ offset) * half, half)
        part = jnp.dot(ref[...], weight_ref[pl.ds(start, half), :], preferred_element_type=jnp.float32)
        if offset == 0:
            total[...] = part
        elif offset < 7:
            total[...] += part
        else:
            value_ref[...] = (total[...] + part).astype(jnp.bfloat16)


def backward_kernel(value_ref, query_ref, key_ref, cot_ref, weights_ref, query_out, key_out):
    scale = HD ** (-0.5)
    for head in range(query_ref.shape[1] // HD):
        columns = slice(head * HD, (head + 1) * HD)
        weights = weights_ref[head]
        prob_grad = lax.dot_general(
            cot_ref[:, columns], value_ref[:, columns], (((1,), (1,)), ((), ())),
            preferred_element_type=jnp.float32,
        )
        centre = jnp.sum(weights * prob_grad, axis=-1, keepdims=True)
        score_grad = (weights * (prob_grad - centre)).astype(jnp.bfloat16)
        query_out[:, columns] = (
            jnp.dot(score_grad, key_ref[:, columns], preferred_element_type=jnp.float32) * scale
        ).astype(jnp.bfloat16)
        key_out[:, columns] = (
            lax.dot_general(
                score_grad, query_ref[:, columns], (((0,), (0,)), ((), ())),
                preferred_element_type=jnp.float32,
            ) * scale
        ).astype(jnp.bfloat16)


def value_parts(info, names, chip_values, mate_values):
    parts = []

    def rows_of(offset, swapped=None):
        values = mate_values.at[offset // 2] if offset % 2 else chip_values[offset // 2]
        if swapped is None:
            return values[...]
        rows = values.shape[0] // 2
        side = (info[2] + swapped) % 2
        return values[pl.ds(pl.multiple_of(side * rows, rows), rows), :]

    for name in names:
        if name == SWAPPED:
            parts.extend(rows_of(offset, 1) for offset in HALVED)
        else:
            parts.append(rows_of(name, 0 if name in HALVED else None))
    return parts


def gradient_first_kernel(info, *refs):
    normed, chip_values, mate_values = refs[:-7], refs[-7:-3], refs[-3]
    sum_ref, right_ref = refs[-2:]
    row = 0
    for part in value_parts(info, LAST, chip_values, mate_values):
        right_ref[row:row + part.shape[0], :] = part
        row += part.shape[0]
    left = jnp.concatenate([ref[...] for ref in normed], axis=0)
    right = jnp.concatenate(value_parts(info, FIRST, chip_values, mate_values), axis=0)
    sum_ref[...] = lax.dot_general(
        left, right, (((0,), (0,)), ((), ())), preferred_element_type=jnp.float32
    )


def gradient_last_kernel(before, right, *refs):
    normed, (out_ref, ready, done) = refs[:-3], refs[-3:]
    left = jnp.concatenate([ref[...] for ref in normed], axis=0)
    blocks, rows, _ = ready.shape
    copies = []
    for block in range(blocks):
        part = slice(block * rows, (block + 1) * rows)
        ready[block] = before[part, :] + lax.dot_general(
            left[:, part], right[...], (((0,), (0,)), ((), ())), preferred_element_type=jnp.float32
        )
        copies.append(
            pltpu.make_async_copy(ready.at[block], out_ref.at[pl.ds(block * rows, rows)], done.at[block])
        )
        copies[-1].start()
    for copy in copies:
        copy.wait()


def shape(dims, dtype=jnp.bfloat16):
    return jax.ShapeDtypeStruct(dims, dtype)


VMEM_LIMIT = 24 * 1024 * 1024
BIG = 56 * 1024 * 1024
SMEM = pl.BlockSpec(memory_space=pltpu.SMEM)
WHOLE = pl.BlockSpec(memory_space=pltpu.VMEM)
ANY = pl.BlockSpec(memory_space=pl.ANY)


def call(kernel, name, out_shape, in_specs, out_specs, scratch=(), limit=VMEM_LIMIT, after=()):
    used = len(in_specs)

    def body(*refs):
        return kernel(*refs[:used], *refs[used + len(after):])

    made = pl.pallas_call(
        body,
        name=name,
        out_shape=out_shape,
        in_specs=list(in_specs) + [ANY] * len(after),
        out_specs=out_specs,
        scratch_shapes=list(scratch),
        cost_estimate=pl.CostEstimate(flops=1, bytes_accessed=1, transcendentals=0),
        compiler_params=pltpu.CompilerParams(vmem_limit_bytes=limit),
    )
    return lambda *args: made(*args, *after)


def across(rows, distance):
    return lax.ppermute(rows, "dp", [(i, i ^ distance) for i in range(8)])


def between_chips(blocks):
    return lax.all_to_all(
        blocks, "dp", split_axis=0, concat_axis=0, tiled=True,
        axis_index_groups=[[0, 2, 4, 6], [1, 3, 5, 7]],
    )


def fast_body(
    patches, norm_gain, value_weight, queries, key_vectors, head_cotangent, image_owner, patch_count
):
    rows, columns = patches.shape
    half = columns // 2
    width = queries.shape[1]
    heads = width // HD
    images = image_owner.shape[1]
    slots = head_cotangent.shape[0]
    device = lax.axis_index("dp").astype(jnp.int32)
    place = [device // 2, device % 2, lax.axis_index("mp").astype(jnp.int32)]
    info = jnp.concatenate([
        jnp.stack(place + [jnp.int32(0)] * (HEADER - 3)),
        lax.dynamic_index_in_dim(image_owner, device, 0, keepdims=False),
        lax.dynamic_index_in_dim(patch_count, device, 0, keepdims=False),
    ])
    flat = (rows, width)

    received = lax.all_to_all(
        head_cotangent.reshape(8, slots // 8, width), "dp", split_axis=0, concat_axis=0, tiled=True
    ).reshape(slots, width)
    two = lax.ppermute(patches, "mp", [(0, 2), (2, 0), (1, 3), (3, 1)])
    one = lax.ppermute(patches, "mp", [(0, 1), (1, 0), (2, 3), (3, 2)])

    weights, gain = call(
        functools.partial(weights_kernel, images), "attention_weights",
        (shape((heads, rows, rows), jnp.float32), shape((8, half), jnp.float32)), [SMEM] + [WHOLE] * 3, (WHOLE, WHOLE),
    )(info, norm_gain.reshape(8, half), queries, key_vectors)
    cotangent, value_rows = call(
        functools.partial(value_kernel, images), "value_rows",
        (shape(flat), shape(flat)), [SMEM, WHOLE, WHOLE], (WHOLE, WHOLE),
    )(info, received, weights)
    middle, first_one, ready = lax.optimization_barrier((patches, one, value_rows))
    passed, _ = lax.optimization_barrier((two, ready))
    near = lax.ppermute(middle, "mp", [(1, 2), (2, 1)])
    far = lax.ppermute(passed, "mp", [(2, 3), (1, 0)])
    chip_values = [value_rows] + [across(value_rows, distance) for distance in (2, 4, 6)]

    block = shape((rows, half))
    stats, arranged = call(
        stats_kernel, "partial_stats", (shape((rows, 128), jnp.float32), shape((4, rows, columns))),
        [SMEM] + [WHOLE] * 3, (WHOLE, WHOLE), after=(value_weight,),
    )(info, middle, passed, first_one)
    *normed, = call(
        norm_kernel, "norm_rows", (block,) * 8 + (shape((rows // 2, half)),) * len(HALVED),
        [SMEM] + [WHOLE] * 5, (WHOLE,) * (8 + len(HALVED)), (pltpu.VMEM((rows, columns), jnp.bfloat16),),
    )(info, stats, gain, arranged, near, far)
    normed, halves = normed[:8], normed[8:]
    packed = call(pack_kernel, "pack_values", shape((4,) + flat), [WHOLE] * 4, WHOLE, after=(normed[1],))(*chip_values)

    mate_values = across(packed, 1)
    mate_rows = across(normed[1], 1)
    values = call(
        project_kernel, "project_values", shape(flat), [SMEM] + [WHOLE] * 9, WHOLE, (pltpu.VMEM(flat, jnp.float32),),
        after=(mate_values, mate_rows),
    )(info, value_weight, *normed)
    query_grad, key_grad = call(
        backward_kernel, "attention_backward", (shape(flat), shape(flat)), [WHOLE] * 5, (WHOLE,) * 2,
    )(values, queries, key_vectors, cotangent, weights)

    moved = {0: normed[0], 1: mate_rows}
    sources = {offset: normed[offset] for offset in range(2, 8)} | dict(zip(HALVED, halves))
    for offset in range(2, 8):
        if offset not in LATE:
            moved[offset] = across(sources[offset], offset)
    swapped = call(pack_kernel, "pack_halves", shape((2, rows // 2, half)), [WHOLE] * 2, WHOLE, after=(values,))(
        *[moved[offset] for offset in HALVED]
    )
    sources[SWAPPED] = swapped.reshape(rows, half)
    held = lax.optimization_barrier([sources[name] for name in LATE] + [values])
    for name, part in zip(LATE, held):
        if name == SWAPPED:
            moved[name] = lax.ppermute(part, "mp", [(0, 1), (1, 0), (2, 3), (3, 2)])
        else:
            moved[name] = across(part, name)

    first, last = [moved[name] for name in FIRST], [moved[name] for name in LAST]
    grad = shape((half, width), jnp.float32)
    partial, last_values = call(
        gradient_first_kernel, "gradient_first", (grad, shape((rows * len(LAST), width))),
        [SMEM] + [WHOLE] * (len(first) + 5), (WHOLE, WHOLE),
    )(info, *first, *chip_values, mate_values)
    blocks = half // 256
    weight_grad = call(
        gradient_last_kernel, "gradient_last", grad, [WHOLE] * (len(last) + 2), ANY,
        (pltpu.VMEM((blocks, 256, width), jnp.float32), pltpu.SemaphoreType.DMA((blocks,))),
        after=(query_grad,),
    )(partial, last_values, *last)
    return weight_grad, query_grad, key_grad


def solution(mesh):
    fast = mesh.shape["dp"] == 8 and mesh.shape["mp"] == 4
    return jax.shard_map(
        fast_body if fast else general_body,
        mesh=mesh,
        in_specs=(
            P("dp", "mp"),
            P(),
            P(None, "mp"),
            P("dp", "mp"),
            P("dp", "mp"),
            P("dp", "mp"),
            P(),
            P(),
        ),
        out_specs=(P("dp", "mp"), P("dp", "mp"), P("dp", "mp")),
        check_vma=False,
    )
```

```python
import functools

import jax
import jax.numpy as jnp
from jax import lax
from jax.experimental import pallas as pl
from jax.experimental.pallas import tpu as pltpu
from jax.sharding import PartitionSpec as P

HD = 128
HEADER = 8
FIRST = (0,6,7,2,4,1)
LAST = (20,3,5)
LATE = (20, 5)
HALVED = (6, 7)
SWAPPED = 20


def normalize(rows, norm_gain):
    values = rows.astype(jnp.float32)
    average = jnp.mean(values, axis=-1, keepdims=True)
    centred = values - average
    variance = jnp.mean(centred * centred, axis=-1, keepdims=True)
    return (centred * lax.rsqrt(variance + 1e-06) * norm_gain).astype(jnp.bfloat16)


def row_plan(image_owner, patch_count, rows_here, capacity, devices):
    device = lax.axis_index("dp")
    own_list = lax.dynamic_index_in_dim(image_owner, device, 0, keepdims=False)
    own_count = lax.dynamic_index_in_dim(patch_count, device, 0, keepdims=False)
    ends = jnp.cumsum(own_count)
    starts = ends - own_count
    row_index = jnp.arange(rows_here, dtype=jnp.int32)
    image_of = jnp.sum((ends[None, :] <= row_index[:, None]).astype(jnp.int32), axis=1)
    picked = image_of[:, None] == jnp.arange(devices, dtype=jnp.int32)[None, :]
    row_owner = jnp.sum(jnp.where(picked, own_list[None, :], 0), axis=1)
    row_start = jnp.sum(jnp.where(picked, starts[None, :], 0), axis=1)
    return image_of, row_owner * capacity + row_index - row_start


def attention_grads(query_rows, key_rows, value_rows, cotangent, segment):
    total, width = query_rows.shape
    heads = width // HD
    scale = HD ** (-0.5)

    def split(rows):
        return rows.reshape(total, heads, HD)

    query, key, value, cot = split(query_rows), split(key_rows), split(value_rows), split(cotangent)
    scores = jnp.einsum("qhd,khd->hqk", query, key, preferred_element_type=jnp.float32) * scale
    allowed = segment[:, None] == segment[None, :]
    scores = jnp.where(allowed[None], scores, -1000000000.0)
    weights = jnp.exp(scores - jnp.max(scores, axis=-1, keepdims=True))
    weights = weights / jnp.sum(weights, axis=-1, keepdims=True)
    value_grad = jnp.einsum(
        "hqk,qhd->khd", weights.astype(jnp.bfloat16), cot, preferred_element_type=jnp.float32
    )
    prob_grad = jnp.einsum("qhd,khd->hqk", cot, value, preferred_element_type=jnp.float32)
    centre = jnp.sum(weights * prob_grad, axis=-1, keepdims=True)
    score_grad = (weights * (prob_grad - centre)).astype(jnp.bfloat16)
    query_grad = jnp.einsum("hqk,khd->qhd", score_grad, key, preferred_element_type=jnp.float32)
    key_grad = jnp.einsum("hqk,qhd->khd", score_grad, query, preferred_element_type=jnp.float32)

    def join(rows):
        return rows.astype(jnp.bfloat16).reshape(total, width)

    return join(value_grad), join(query_grad * scale), join(key_grad * scale)


def general_body(
    patches, norm_gain, value_weight, queries, key_vectors, head_cotangent, image_owner, patch_count
):
    devices = lax.axis_size("dp")
    rows_here = patches.shape[0]
    width = queries.shape[1]
    capacity = head_cotangent.shape[0] // devices
    segment, index = row_plan(image_owner, patch_count, rows_here, capacity, devices)
    slots = lax.all_to_all(
        head_cotangent.reshape(devices, capacity, width), "dp", split_axis=0, concat_axis=0, tiled=True
    )
    cotangent = slots.reshape(devices * capacity, width)[index]
    normed = normalize(lax.all_gather(patches, "mp", axis=1, tiled=True), norm_gain)
    values = jnp.dot(normed, value_weight, preferred_element_type=jnp.float32).astype(jnp.bfloat16)
    value_rows, query_grad, key_grad = attention_grads(
        queries, key_vectors, values, cotangent, segment
    )
    all_value_rows = lax.all_gather(value_rows, "dp", axis=0, tiled=True)
    columns = jnp.swapaxes(normed.reshape(rows_here, devices, -1), 0, 1)
    columns = lax.all_to_all(columns, "dp", split_axis=0, concat_axis=0, tiled=True)
    columns = columns.reshape(devices * rows_here, -1)
    weight_grad = lax.dot_general(
        columns, all_value_rows, (((0,), (0,)), ((), ())), preferred_element_type=jnp.float32
    )
    return weight_grad, query_grad, key_grad


def image_plan(info, row, images, capacity):
    image = jnp.zeros(row.shape, jnp.int32)
    position = jnp.zeros(row.shape, jnp.int32)
    start = jnp.int32(0)
    for index in range(images):
        end = start + info[HEADER + images + index]
        inside = (row >= start) & (row < end)
        image = jnp.where(inside, index, image)
        position = jnp.where(inside, info[HEADER + index] * capacity + row - start, position)
        start = end
    return image, position


def weights_kernel(images, info, gain_in, query_ref, key_ref, weights_ref, gain_ref):
    gain_ref[...] = gain_in[...]
    rows, width = query_ref.shape
    down = lax.broadcasted_iota(jnp.int32, (rows, rows), 0)
    across = lax.broadcasted_iota(jnp.int32, (rows, rows), 1)
    allowed = image_plan(info, down, images, 1)[0] == image_plan(info, across, images, 1)[0]
    for head in range(width // HD):
        columns = slice(head * HD, (head + 1) * HD)
        scores = lax.dot_general(
            query_ref[:, columns], key_ref[:, columns], (((1,), (1,)), ((), ())),
            preferred_element_type=jnp.float32,
        ) * (HD ** (-0.5))
        scores = jnp.where(allowed, scores, -1000000000.0)
        weights = jnp.exp(scores - jnp.max(scores, axis=-1, keepdims=True))
        weights_ref[head] = weights / jnp.sum(weights, axis=-1, keepdims=True)


def value_kernel(images, info, slots_ref, weights_ref, cot_ref, value_ref):
    slots, width = slots_ref.shape
    rows = cot_ref.shape[0]
    row = lax.broadcasted_iota(jnp.int32, (rows, slots), 0)
    _, position = image_plan(info, row, images, slots // images)
    pick = position == lax.broadcasted_iota(jnp.int32, (rows, slots), 1)
    pick = jnp.where(pick, 1.0, 0.0).astype(jnp.bfloat16)
    cot_ref[...] = jnp.dot(
        pick, slots_ref[...], preferred_element_type=jnp.float32
    ).astype(jnp.bfloat16)
    for head in range(width // HD):
        columns = slice(head * HD, (head + 1) * HD)
        value_ref[:, columns] = lax.dot_general(
            weights_ref[head].astype(jnp.bfloat16), cot_ref[:, columns], (((0,), (0,)), ((), ())),
            preferred_element_type=jnp.float32,
        ).astype(jnp.bfloat16)


def spread_of(values):
    mean = jnp.sum(values, axis=-1, keepdims=True) * (1.0 / values.shape[1])
    centred = values - mean
    return mean, jnp.sum(centred * centred, axis=-1, keepdims=True)


def stats_kernel(info, own, two, one, stats_ref, arranged):
    for index, ref in enumerate((own, one, two)):
        arranged[index ^ info[2]] = ref[...]
    rows = own.shape[0]
    lane = lax.broadcasted_iota(jnp.int32, (rows, 128), 1)
    table = jnp.zeros((rows, 128), jnp.float32)
    for index, ref in enumerate((own, one, two)):
        mean, spread = spread_of(ref[...].astype(jnp.float32))
        table = jnp.where(lane == index, mean, table)
        table = jnp.where(lane == index + 3, spread, table)
    stats_ref[...] = table


def norm_kernel(info, stats_ref, gain_ref, arranged, near, far, *rest):
    outs, halves, last_ref = rest[:8], rest[8:-1], rest[-1]
    device, layer = 2 * info[0] + info[1], info[2]
    rows, half = outs[0].shape
    last = near[...].astype(jnp.float32) + far[...].astype(jnp.float32)
    last_ref[...] = last.astype(jnp.bfloat16)
    columns = 8 * half
    last_mean, last_spread = spread_of(last)
    table = stats_ref[...]
    means = [table[:, index:index + 1] for index in range(3)] + [last_mean]
    mean = sum(means) * 0.25
    shift = sum((part - mean) * (part - mean) for part in means) * (2 * half)
    spread = table[:, 3:4] + table[:, 4:5] + table[:, 5:6] + last_spread + shift
    rstd = lax.rsqrt(spread * (1.0 / columns) + 1e-06)
    for offset, out in enumerate(outs):
        block = device ^ offset
        start = pl.multiple_of((block % 2) * half, half)
        origin = block // 2
        values = jnp.where(
            (origin ^ layer) == 3, last_ref[:, pl.ds(start, half)], arranged[origin, :, pl.ds(start, half)]
        )
        gain = gain_ref[pl.ds(block, 1), :]
        out[...] = ((values.astype(jnp.float32) - mean) * rstd * gain).astype(jnp.bfloat16)
    first = pl.multiple_of((layer % 2) * (rows // 2), rows // 2)
    for offset, ref in zip(HALVED, halves):
        ref[...] = outs[offset][pl.ds(first, rows // 2), :]


def pack_kernel(*refs):
    for index, ref in enumerate(refs[:-1]):
        refs[-1][index] = ref[...]


def project_kernel(info, weight_ref, *refs):
    normed, (value_ref, total) = refs[:8], refs[8:]
    device = 2 * info[0] + info[1]
    half = normed[0].shape[1]
    for offset, ref in enumerate(normed):
        start = pl.multiple_of((device ^ offset) * half, half)
        part = jnp.dot(ref[...], weight_ref[pl.ds(start, half), :], preferred_element_type=jnp.float32)
        if offset == 0:
            total[...] = part
        elif offset < 7:
            total[...] += part
        else:
            value_ref[...] = (total[...] + part).astype(jnp.bfloat16)


def backward_kernel(value_ref, query_ref, key_ref, cot_ref, weights_ref, query_out, key_out):
    scale = HD ** (-0.5)
    for head in range(query_ref.shape[1] // HD):
        columns = slice(head * HD, (head + 1) * HD)
        weights = weights_ref[head]
        prob_grad = lax.dot_general(
            cot_ref[:, columns], value_ref[:, columns], (((1,), (1,)), ((), ())),
            preferred_element_type=jnp.float32,
        )
        centre = jnp.sum(weights * prob_grad, axis=-1, keepdims=True)
        score_grad = (weights * (prob_grad - centre)).astype(jnp.bfloat16)
        query_out[:, columns] = (
            jnp.dot(score_grad, key_ref[:, columns], preferred_element_type=jnp.float32) * scale
        ).astype(jnp.bfloat16)
        key_out[:, columns] = (
            lax.dot_general(
                score_grad, query_ref[:, columns], (((0,), (0,)), ((), ())),
                preferred_element_type=jnp.float32,
            ) * scale
        ).astype(jnp.bfloat16)


def value_parts(info, names, chip_values, mate_values):
    parts = []

    def rows_of(offset, swapped=None):
        values = mate_values.at[offset // 2] if offset % 2 else chip_values[offset // 2]
        if swapped is None:
            return values[...]
        rows = values.shape[0] // 2
        side = (info[2] + swapped) % 2
        return values[pl.ds(pl.multiple_of(side * rows, rows), rows), :]

    for name in names:
        if name == SWAPPED:
            parts.extend(rows_of(offset, 1) for offset in HALVED)
        else:
            parts.append(rows_of(name, 0 if name in HALVED else None))
    return parts


def gradient_first_kernel(info, *refs):
    normed, chip_values, mate_values = refs[:-7], refs[-7:-3], refs[-3]
    sum_ref, right_ref = refs[-2:]
    row = 0
    for part in value_parts(info, LAST, chip_values, mate_values):
        right_ref[row:row + part.shape[0], :] = part
        row += part.shape[0]
    left = jnp.concatenate([ref[...] for ref in normed], axis=0)
    right = jnp.concatenate(value_parts(info, FIRST, chip_values, mate_values), axis=0)
    sum_ref[...] = lax.dot_general(
        left, right, (((0,), (0,)), ((), ())), preferred_element_type=jnp.float32
    )


def gradient_last_kernel(before, right, *refs):
    normed, (out_ref, ready, done) = refs[:-3], refs[-3:]
    left = jnp.concatenate([ref[...] for ref in normed], axis=0)
    blocks, rows, _ = ready.shape
    copies = []
    for block in range(blocks):
        part = slice(block * rows, (block + 1) * rows)
        ready[block] = before[part, :] + lax.dot_general(
            left[:, part], right[...], (((0,), (0,)), ((), ())), preferred_element_type=jnp.float32
        )
        copies.append(
            pltpu.make_async_copy(ready.at[block], out_ref.at[pl.ds(block * rows, rows)], done.at[block])
        )
        copies[-1].start()
    for copy in copies:
        copy.wait()


def shape(dims, dtype=jnp.bfloat16):
    return jax.ShapeDtypeStruct(dims, dtype)


VMEM_LIMIT = 24 * 1024 * 1024
BIG = 56 * 1024 * 1024
SMEM = pl.BlockSpec(memory_space=pltpu.SMEM)
WHOLE = pl.BlockSpec(memory_space=pltpu.VMEM)
ANY = pl.BlockSpec(memory_space=pl.ANY)


def call(kernel, name, out_shape, in_specs, out_specs, scratch=(), limit=VMEM_LIMIT, after=()):
    used = len(in_specs)

    def body(*refs):
        return kernel(*refs[:used], *refs[used + len(after):])

    made = pl.pallas_call(
        body,
        name=name,
        out_shape=out_shape,
        in_specs=list(in_specs) + [ANY] * len(after),
        out_specs=out_specs,
        scratch_shapes=list(scratch),
        cost_estimate=pl.CostEstimate(flops=1, bytes_accessed=1, transcendentals=0),
        compiler_params=pltpu.CompilerParams(vmem_limit_bytes=limit),
    )
    return lambda *args: made(*args, *after)


def across(rows, distance):
    return lax.ppermute(rows, "dp", [(i, i ^ distance) for i in range(8)])


def between_chips(blocks):
    return lax.all_to_all(
        blocks, "dp", split_axis=0, concat_axis=0, tiled=True,
        axis_index_groups=[[0, 2, 4, 6], [1, 3, 5, 7]],
    )


def fast_body(
    patches, norm_gain, value_weight, queries, key_vectors, head_cotangent, image_owner, patch_count
):
    rows, columns = patches.shape
    half = columns // 2
    width = queries.shape[1]
    heads = width // HD
    images = image_owner.shape[1]
    slots = head_cotangent.shape[0]
    device = lax.axis_index("dp").astype(jnp.int32)
    place = [device // 2, device % 2, lax.axis_index("mp").astype(jnp.int32)]
    info = jnp.concatenate([
        jnp.stack(place + [jnp.int32(0)] * (HEADER - 3)),
        lax.dynamic_index_in_dim(image_owner, device, 0, keepdims=False),
        lax.dynamic_index_in_dim(patch_count, device, 0, keepdims=False),
    ])
    flat = (rows, width)

    received = lax.all_to_all(
        head_cotangent.reshape(8, slots // 8, width), "dp", split_axis=0, concat_axis=0, tiled=True
    ).reshape(slots, width)
    two = lax.ppermute(patches, "mp", [(0, 2), (2, 0), (1, 3), (3, 1)])
    one = lax.ppermute(patches, "mp", [(0, 1), (1, 0), (2, 3), (3, 2)])

    weights, gain = call(
        functools.partial(weights_kernel, images), "attention_weights",
        (shape((heads, rows, rows), jnp.float32), shape((8, half), jnp.float32)), [SMEM] + [WHOLE] * 3, (WHOLE, WHOLE),
    )(info, norm_gain.reshape(8, half), queries, key_vectors)
    cotangent, value_rows = call(
        functools.partial(value_kernel, images), "value_rows",
        (shape(flat), shape(flat)), [SMEM, WHOLE, WHOLE], (WHOLE, WHOLE),
    )(info, received, weights)
    middle, first_one, ready = lax.optimization_barrier((patches, one, value_rows))
    passed, _ = lax.optimization_barrier((two, ready))
    near = lax.ppermute(middle, "mp", [(1, 2), (2, 1)])
    far = lax.ppermute(passed, "mp", [(2, 3), (1, 0)])
    chip_values = [value_rows] + [across(value_rows, distance) for distance in (2, 4, 6)]

    block = shape((rows, half))
    stats, arranged = call(
        stats_kernel, "partial_stats", (shape((rows, 128), jnp.float32), shape((4, rows, columns))),
        [SMEM] + [WHOLE] * 3, (WHOLE, WHOLE), after=(value_weight,),
    )(info, middle, passed, first_one)
    *normed, = call(
        norm_kernel, "norm_rows", (block,) * 8 + (shape((rows // 2, half)),) * len(HALVED),
        [SMEM] + [WHOLE] * 5, (WHOLE,) * (8 + len(HALVED)), (pltpu.VMEM((rows, columns), jnp.bfloat16),),
    )(info, stats, gain, arranged, near, far)
    normed, halves = normed[:8], normed[8:]
    packed = call(pack_kernel, "pack_values", shape((4,) + flat), [WHOLE] * 4, WHOLE, after=(normed[1],))(*chip_values)

    mate_values = across(packed, 1)
    mate_rows = across(normed[1], 1)
    values = call(
        project_kernel, "project_values", shape(flat), [SMEM] + [WHOLE] * 9, WHOLE, (pltpu.VMEM(flat, jnp.float32),),
        after=(mate_values, mate_rows),
    )(info, value_weight, *normed)
    query_grad, key_grad = call(
        backward_kernel, "attention_backward", (shape(flat), shape(flat)), [WHOLE] * 5, (WHOLE,) * 2,
    )(values, queries, key_vectors, cotangent, weights)

    moved = {0: normed[0], 1: mate_rows}
    sources = {offset: normed[offset] for offset in range(2, 8)} | dict(zip(HALVED, halves))
    for offset in range(2, 8):
        if offset not in LATE:
            moved[offset] = across(sources[offset], offset)
    swapped = call(pack_kernel, "pack_halves", shape((2, rows // 2, half)), [WHOLE] * 2, WHOLE, after=(values,))(
        *[moved[offset] for offset in HALVED]
    )
    sources[SWAPPED] = swapped.reshape(rows, half)
    held = lax.optimization_barrier([sources[name] for name in LATE] + [values])
    for name, part in zip(LATE, held):
        if name == SWAPPED:
            moved[name] = lax.ppermute(part, "mp", [(0, 1), (1, 0), (2, 3), (3, 2)])
        else:
            moved[name] = across(part, name)

    first, last = [moved[name] for name in FIRST], [moved[name] for name in LAST]
    grad = shape((half, width), jnp.float32)
    partial, last_values = call(
        gradient_first_kernel, "gradient_first", (grad, shape((rows * len(LAST), width))),
        [SMEM] + [WHOLE] * (len(first) + 5), (WHOLE, WHOLE),
    )(info, *first, *chip_values, mate_values)
    blocks = half // 256
    weight_grad = call(
        gradient_last_kernel, "gradient_last", grad, [WHOLE] * (len(last) + 2), ANY,
        (pltpu.VMEM((blocks, 256, width), jnp.float32), pltpu.SemaphoreType.DMA((blocks,))),
        after=(query_grad,),
    )(partial, last_values, *last)
    return weight_grad, query_grad, key_grad


def solution(mesh):
    fast = mesh.shape["dp"] == 8 and mesh.shape["mp"] == 4
    return jax.shard_map(
        fast_body if fast else general_body,
        mesh=mesh,
        in_specs=(
            P("dp", "mp"),
            P(),
            P(None, "mp"),
            P("dp", "mp"),
            P("dp", "mp"),
            P("dp", "mp"),
            P(),
            P(),
        ),
        out_specs=(P("dp", "mp"), P("dp", "mp"), P("dp", "mp")),
        check_vma=False,
    )
```
